256 devices in a mesh: sy: 8 (over y, x_lo), sx: 16 (over z, core), dp: 2 (over x_hi).
Axes of the slice: x: 4 (x_hi: 2, x_lo: 2; x = x_hi * 2 + x_lo), y: 4, z: 8, core: 2. Of those that a mesh axis runs over, the one named last changes fastest.
Arguments:
- tokens: bfloat16 [2, 128, 512, 512], P('dp', 'sy', 'sx'), may hold values from -6 to 6
- cotangent: bfloat16 [2, 128, 512, 512], P('dp', 'sy', 'sx'), may hold values from -6 to 6
- w_qkv: bfloat16 [512, 1536], replicated, may hold values from -0.25 to 0.25
- w_proj: bfloat16 [512, 512], replicated, may hold values from -0.25 to 0.25
- logit_scale: float32 [16], replicated, may hold values from 2 to 20
- w_router: bfloat16 [512, 32], replicated, may hold values from -0.25 to 0.25
- w_up: bfloat16 [32, 512, 2048], P('sx'), may hold values from -0.25 to 0.25
- w_down: bfloat16 [32, 2048, 512], P('sx'), may hold values from -0.125 to 0.125
- expert_ids: int32 [2, 8, 16, 512, 1], P('dp', 'sy', 'sx'), may hold values from 0 to 31; in each aligned block of 512 rows (0 to 511, 512 to 1023, ..., all dimensions but the last counted through in order) at most 32 rows name the same one
Outputs:
- mixed: bfloat16 [2, 128, 512, 512], P('dp', 'sy', 'sx')
- grad_up: float32 [32, 512, 2048], P('sx', None, ('sy', 'dp'))
- grad_down: float32 [32, 2048, 512], P('sx', ('sy', 'dp'))
The draws below stay inside these ranges and needn't reach their ends.
Inputs may be any that keep to these rules, and one draw needn't show every extreme that they name: `expert_ids`: among the tokens of one device no expert is named by more than 32 tokens.
All inputs are finite; a program needn't handle non-finite values.
Results may differ from the reference program's by a relative error of at most 0.024.
Values may be sent and summed in bfloat16 or wider, within the bound.
A program may use at most 128 MiB of HBM per device.

```python
import math
import jax
import jax.numpy as jnp
import numpy as np
from jax import lax

D = 512
HEADS = 16
FF = 2048
WIN = 16
SHIFT = 8
TH = 16
TW = 32
EXPERTS = 32
TOK_DEV = 512
CAP = 32
SCENES = 2
GRID_Y = 8
GRID_X = 16
MAP_H = 128
MAP_W = 512
N_SY = 8
N_SX = 16
N_DP = 2


def shard_levels(own_key, dims, split, least, high):
    loudness, own = 1.0, jax.random.fold_in(own_key, 6)
    for dim, blocks in split:
        heights = jnp.exp(jax.random.uniform(jax.random.fold_in(own, dim), (blocks,), jnp.float32, least / len(split), high / len(split)))
        loudness = loudness * jnp.repeat(heights, dims[dim] // blocks).reshape([-1 if axis == dim else 1 for axis in range(len(dims))])
    return loudness


def deal_out(rng, own, number, rows, number_of, top, reach, skew):
    sequence = jax.random.permutation(rng, number_of)
    heavy_load, usual = portions_of(number_of, rows * top, reach, skew, True), portions_of(number_of, rows * top, reach, skew, False)
    places = jnp.arange(number_of)

    def named(sizes, rotation):
        used = int((sizes > 0).sum())
        fixed = max(1, used // 4)
        shifted = fixed + (places - fixed + rotation * (used - fixed)) % max(1, number_of - fixed)
        return jnp.zeros((number_of,), jnp.int32).at[sequence[jnp.where(places < fixed, places, shifted)]].set(jnp.asarray(sizes, jnp.int32))

    sizes = jnp.where(number % 4 == 0, named(heavy_load, number // 4), named(usual, number - number // 4 - 1))
    mixed = jax.random.permutation(jax.random.fold_in(own, 3), number_of)
    giver, sink = mixed[0:number_of // 2 * 2:2], mixed[1:number_of // 2 * 2:2]
    room = jnp.minimum(sizes[giver] - 1, reach - sizes[sink]) // 2
    room = jnp.where((giver == sequence[0]) | (sink == sequence[0]) | (sizes[sink] == 0), 0, jnp.maximum(room, 0))
    shifted = jax.random.randint(jax.random.fold_in(own, 4), (number_of // 2,), 0, 1 << 20) % (room + 1)
    sizes = sizes.at[giver].add(-shifted).at[sink].add(shifted)
    items = jnp.searchsorted(jnp.cumsum(sizes), jnp.arange(rows * top), side="right").astype(jnp.int32)
    listing = items.reshape(top, rows).T
    listing = listing[jax.random.permutation(jax.random.fold_in(own, 1), rows)]
    rotation = jax.random.randint(jax.random.fold_in(own, 2), (rows, 1), 0, top)
    return jnp.take_along_axis(listing, (jnp.arange(top)[None, :] + rotation) % top, axis=1)


def portions_of(amount, total, most, skew, full):
    loads = [(1 << 20) // math.isqrt(grade ** skew) + 1 for grade in range(1, amount + 1)]
    largest = most if full else min(most, max(-(-total // amount), total * loads[0] // sum(loads)))
    least = 1 if total - largest >= amount - 1 else 0
    given, surplus = [largest] + [least] * (amount - 1), total - largest - least * (amount - 1)
    while surplus > 0:
        candidates = [i for i in range(1, amount) if given[i] < largest] or [i for i in range(1, amount) if given[i] < most]
        whole, remaining = sum([loads[i] for i in candidates]), surplus
        for i in candidates:
            extra = min(most - given[i], max(1, remaining * loads[i] // whole), surplus)
            given[i] = given[i] + extra
            surplus = surplus - extra
    return np.array(given)


def scatter_about(stream_key, shape, deviation, limit, shards=(), kind=jnp.bfloat16):
    loudness = shard_levels(stream_key, shape, shards, -0.22, 0.18) if shards else 1.0
    drawn = jax.random.normal(stream_key, shape, jnp.float32) * deviation * loudness
    return jnp.minimum(jnp.maximum(drawn, -limit), limit).astype(kind)


def setup_inputs(seed: int = 0) -> dict:
    seeds = jax.random.split(jax.random.key(seed), 10)
    tokens = scatter_about(seeds[0], (SCENES, MAP_H, MAP_W, D), 1.0, 6.0, ((0, 2), (1, 8), (2, 16)))
    cotangent = scatter_about(seeds[1], (SCENES, MAP_H, MAP_W, D), 1.0, 6.0, ((0, 2), (1, 8), (2, 16)))
    w_qkv = scatter_about(seeds[2], (D, 3 * D), D ** -0.5, 0.25)
    w_proj = scatter_about(seeds[3], (D, D), D ** -0.5, 0.25)
    logit_scale = jnp.clip(jnp.exp(jax.random.uniform(seeds[4], (HEADS,), jnp.float32, math.log(2.0), math.log(20.0))), 2.0, 20.0)
    w_router = scatter_about(seeds[5], (D, EXPERTS), D ** -0.5, 0.25)
    w_up = scatter_about(seeds[6], (EXPERTS, D, FF), D ** -0.5, 0.25, ((0, 16),))
    w_down = scatter_about(seeds[7], (EXPERTS, FF, D), FF ** -0.5, 0.125, ((0, 16),))
    expert_ids_keys = jax.random.split(jax.random.fold_in(seeds[8], 1), SCENES * GRID_Y * GRID_X * TOK_DEV // TOK_DEV)
    expert_ids_turns = jax.random.permutation(jax.random.fold_in(seeds[8], 3), SCENES * GRID_Y * GRID_X * TOK_DEV // TOK_DEV)
    expert_ids = jax.vmap(lambda own, number: deal_out(jax.random.fold_in(seeds[8], 2), own, number, TOK_DEV, EXPERTS, 1, CAP, 2))(expert_ids_keys, expert_ids_turns).reshape((SCENES, GRID_Y, GRID_X, TOK_DEV, 1))
    return dict(tokens=tokens, cotangent=cotangent, w_qkv=w_qkv, w_proj=w_proj, logit_scale=logit_scale, w_router=w_router, w_up=w_up, w_down=w_down, expert_ids=expert_ids)


def layer_norm(values_in):
    mean = lax.optimization_barrier(jnp.mean(values_in, axis=-1, keepdims=True))
    centred = values_in - mean
    return centred * lax.rsqrt(lax.optimization_barrier(jnp.mean(centred * centred, axis=-1, keepdims=True)) + 1e-05)

def attend(windows, labels, w_qkv, w_proj, logit_scale):
    count, length, width = windows.shape
    heads = logit_scale.shape[0]
    head_dim = width // heads
    normed = layer_norm(windows.astype(jnp.float32)).astype(jnp.bfloat16)
    mixed = jnp.dot(normed.reshape(count * length, width), w_qkv, preferred_element_type=jnp.float32)
    mixed = mixed.reshape(count, length, 3, heads, head_dim)
    query = mixed[:, :, 0]
    keys = mixed[:, :, 1]
    values = mixed[:, :, 2].astype(jnp.bfloat16)
    query = query / jnp.maximum(jnp.sqrt(lax.optimization_barrier(jnp.sum(query * query, axis=-1, keepdims=True))), 4.0)
    keys = keys / jnp.maximum(jnp.sqrt(lax.optimization_barrier(jnp.sum(keys * keys, axis=-1, keepdims=True))), 4.0)
    scores = jnp.einsum('wqhc,wkhc->whqk', query, keys, precision=lax.Precision.HIGHEST)
    scores = scores * logit_scale[None, :, None, None]
    allowed = labels[:, None, :, None] == labels[:, None, None, :]
    weights = jnp.where(allowed, jnp.exp(scores), 0.0)
    probs = (weights / lax.optimization_barrier(jnp.sum(weights, axis=-1, keepdims=True))).astype(jnp.bfloat16)
    joined = jnp.einsum('whqk,wkhc->wqhc', probs.astype(jnp.float32), values.astype(jnp.float32))
    joined = joined.astype(jnp.bfloat16).reshape(count * length, width)
    result = jnp.dot(joined, w_proj, preferred_element_type=jnp.float32).astype(jnp.bfloat16)
    return result.reshape(count, length, width)

def to_devices(field):
    moved = field.reshape(SCENES, N_SY, TH, N_SX, TW, D).transpose(0, 1, 3, 2, 4, 5)
    return moved.reshape(SCENES * N_SY * N_SX * TOK_DEV, D)

def reference(tokens, cotangent, w_qkv, w_proj, logit_scale, w_router, w_up, w_down, expert_ids):
    rows_h = MAP_H // WIN
    cols_w = MAP_W // WIN
    length = WIN * WIN
    rolled = jnp.roll(tokens, (-SHIFT, -SHIFT), (1, 2))
    windows = rolled.reshape(SCENES, rows_h, WIN, cols_w, WIN, D).transpose(0, 1, 3, 2, 4, 5)
    windows = windows.reshape(SCENES * rows_h, cols_w, length, D)
    row_label = (jnp.arange(MAP_H) >= MAP_H - SHIFT).astype(jnp.int32)
    col_label = (jnp.arange(MAP_W) >= MAP_W - SHIFT).astype(jnp.int32)
    label_map = row_label[:, None] * 2 + col_label[None, :]
    label_win = label_map.reshape(rows_h, WIN, cols_w, WIN).transpose(0, 2, 1, 3).reshape(rows_h, cols_w, length)
    label_all = jnp.tile(label_win, (SCENES, 1, 1))
    attended = lax.map(lambda pair: attend(pair[0], pair[1], w_qkv, w_proj, logit_scale), (windows, label_all))
    attended = attended.reshape(SCENES, rows_h, cols_w, WIN, WIN, D).transpose(0, 1, 3, 2, 4, 5)
    attended = jnp.roll(attended.reshape(SCENES, MAP_H, MAP_W, D), (SHIFT, SHIFT), (1, 2))
    resid = tokens.astype(jnp.float32) + attended.astype(jnp.float32)
    flat = to_devices(resid)
    cot_flat = to_devices(cotangent)
    total = flat.shape[0]
    ids = expert_ids.reshape(-1).astype(jnp.int32)
    normed = layer_norm(flat).astype(jnp.bfloat16)
    logits = jnp.dot(normed, w_router, preferred_element_type=jnp.float32)
    onehot = ids[:, None] == jnp.arange(EXPERTS, dtype=jnp.int32)[None, :]
    gate = jax.nn.sigmoid(lax.optimization_barrier(jnp.sum(jnp.where(onehot, logits, 0.0), axis=-1)))
    grad_out = (gate[:, None] * cot_flat.astype(jnp.float32)).astype(jnp.bfloat16)
    counts = lax.optimization_barrier(jnp.sum(onehot.astype(jnp.int32), axis=0)).astype(jnp.int32)
    starts = (jnp.cumsum(counts) - counts).astype(jnp.int32)
    order = jnp.argsort(ids, stable=True).astype(jnp.int32)
    most = N_SY * N_SX * N_DP * CAP
    pad_rows = jnp.zeros((most, D), jnp.bfloat16)
    sorted_in = jnp.concatenate([normed[order], pad_rows], 0)
    sorted_grad = jnp.concatenate([grad_out[order], pad_rows], 0)

    def expert(index):
        start = starts[index]
        valid = (jnp.arange(most, dtype=jnp.int32) < counts[index])[:, None]
        rows_in = jnp.where(valid, lax.dynamic_slice_in_dim(sorted_in, start, most, 0), jnp.zeros((), jnp.bfloat16))
        rows_grad = jnp.where(valid, lax.dynamic_slice_in_dim(sorted_grad, start, most, 0), jnp.zeros((), jnp.bfloat16))
        act = jnp.dot(rows_in, w_up[index], preferred_element_type=jnp.float32)
        hidden = jax.nn.gelu(act).astype(jnp.bfloat16)
        expert_out = jnp.dot(hidden, w_down[index], preferred_element_type=jnp.float32).astype(jnp.bfloat16)
        grad_down_e = jnp.dot(hidden.T, rows_grad, preferred_element_type=jnp.float32)
        grad_hidden = jnp.dot(rows_grad, w_down[index].T, preferred_element_type=jnp.float32)
        grad_act = jax.vjp(jax.nn.gelu, act)[1](grad_hidden)[0].astype(jnp.bfloat16)
        grad_up_e = jnp.dot(rows_in.T, grad_act, preferred_element_type=jnp.float32)
        return (expert_out, grad_up_e, grad_down_e)
    outs, grad_up, grad_down = lax.map(expert, jnp.arange(EXPERTS, dtype=jnp.int32))
    sorted_ids = ids[order]
    position = jnp.arange(total, dtype=jnp.int32) - starts[sorted_ids]
    picked = outs[sorted_ids, position]
    moe = jnp.zeros((total, D), jnp.bfloat16).at[order].set(picked)
    result = (flat + gate[:, None] * moe.astype(jnp.float32)).astype(jnp.bfloat16)
    mixed = result.reshape(SCENES, N_SY, N_SX, TH, TW, D).transpose(0, 1, 3, 2, 4, 5)
    mixed = mixed.reshape(SCENES, MAP_H, MAP_W, D)
    return (mixed, grad_up, grad_down)
```

```python
import jax
import jax.numpy as jnp
from jax import lax
from jax.experimental import pallas as pl
from jax.experimental.pallas import tpu as pltpu
from jax.sharding import PartitionSpec as P

WIN = 16
SHIFT = 8
MESH = pl.DeviceIdType.MESH
BF16 = jnp.bfloat16
F32 = jnp.float32


class RingHalf:
    def __init__(self, src, here_a, here_b, to_a, to_b, bufs1, bufs2, hold, out, sems):
        self.src = src
        self.pa, self.pb = here_a, here_b
        self.to_a, self.to_b = to_a, to_b
        self.bufs1, self.bufs2 = bufs1, bufs2
        self.hold = hold
        self.out = out
        self.s1, self.r1, self.s2, self.r2 = sems
        self.order = [lax.rem(here_b + d, 4) for d in (2, 1, 3, 0)]
        self.sent = []

    def copy1(self, ref, kind, way, k):
        copy = pltpu.make_async_remote_copy(
            src_ref=ref,
            dst_ref=self.bufs1.at[kind, way, k],
            send_sem=self.s1.at[kind, way, k],
            recv_sem=self.r1.at[kind, way, k],
            device_id=self.to_a[way],
            device_id_type=MESH,
        )
        return copy

    def copy2(self, ref, kind, way):
        return pltpu.make_async_remote_copy(
            src_ref=ref,
            dst_ref=self.bufs2.at[kind, way],
            send_sem=self.s2.at[kind, way],
            recv_sem=self.r2.at[kind, way],
            device_id=self.to_b[way],
            device_id_type=MESH,
        )

    def start(self, copy):
        copy.start()
        self.sent.append(copy)

    def ahead(self, way):
        return lax.rem(self.pa + (1 if way == 0 else 3), 4)

    def send_far(self, k):
        for way in range(2):
            ref = self.src(way, lax.rem(self.pa + 2, 4), self.order[k])
            self.start(self.copy1(ref, 0, way, k))

    def send_raw(self, k):
        for way in range(2):
            ref = self.src(1 - way, self.ahead(way), self.order[k])
            self.start(self.copy1(ref, 1, way, k))

    def pass_on(self, k):
        for way in range(2):
            got = self.bufs1.at[0, way, k]
            mine = self.src(way, self.ahead(way), self.order[k])
            self.copy1(mine, 0, way, k).wait_recv()
            got[...] = (got[...].astype(F32) + mine[...].astype(F32)).astype(BF16)
            self.start(self.copy1(got, 2, way, k))

    def close1(self, k):
        for e in range(2):
            raw, acc = self.bufs1.at[1, 1 - e, k], self.bufs1.at[2, e, k]
            mine = self.src(e, self.pa, self.order[k])
            self.copy1(raw, 1, 1 - e, k).wait_recv()
            self.copy1(acc, 2, e, k).wait_recv()
            total = mine[...].astype(F32) + raw[...].astype(F32) + acc[...].astype(F32)
            if k < 3:
                self.hold[k, e] = total.astype(BF16)
            else:
                self.out[e] = total
        if k == 0:
            for way in range(2):
                self.start(self.copy2(self.hold.at[0, way], 0, way))
        elif k == 1:
            self.start(self.copy2(self.hold.at[1, 1], 1, 0))
        elif k == 2:
            self.start(self.copy2(self.hold.at[2, 0], 1, 1))

    def pass_on2(self):
        for way in range(2):
            got = self.bufs2.at[0, way]
            self.copy2(got, 0, way).wait_recv()
            got[...] = (got[...].astype(F32) + self.hold[1 + way, way].astype(F32)).astype(BF16)
            self.start(self.copy2(got, 2, way))

    def close2(self):
        for e in range(2):
            raw, acc = self.bufs2.at[1, 1 - e], self.bufs2.at[2, e]
            self.copy2(raw, 1, 1 - e).wait_recv()
            self.copy2(acc, 2, e).wait_recv()
            self.out[e] = self.out[e] + raw[...].astype(F32) + acc[...].astype(F32)

    def finish(self):
        for copy in self.sent:
            copy.wait_send()


def ring_places():
    sy, dp = lax.axis_index("sy"), lax.axis_index("dp")
    y, x = sy // 2, dp * 2 + lax.rem(sy, 2)
    to_x, to_y = [], []
    for step in (1, 3):
        nx, ny = lax.rem(x + step, 4), lax.rem(y + step, 4)
        to_x.append({"sy": y * 2 + lax.rem(nx, 2), "dp": nx // 2})
        to_y.append({"sy": ny * 2 + lax.rem(x, 2)})
    return x, y, to_x, to_y


def shard_of(x, y):
    return y * 4 + lax.rem(x, 2) * 2 + x // 2


def greet(targets):
    barrier = pltpu.get_barrier_semaphore()
    for target in targets:
        pl.semaphore_signal(barrier, inc=1, device_id=target, device_id_type=MESH)
    pl.semaphore_wait(barrier, len(targets))


def reduce_kernel(up_ref, down_ref, oup_ref, odown_ref, u1, u2, uh, d1, d2, dh, *sems):
    x, y, to_x, to_y = ring_places()
    greet(to_x + to_y)

    def up_src(e, ix, iy):
        col = pl.multiple_of(shard_of(ix, iy) * 128, 128)
        return up_ref.at[e, :, pl.ds(col, 128)]

    def down_src(e, iy, ix):
        row = pl.multiple_of(shard_of(ix, iy) * 128, 128)
        return down_ref.at[e, pl.ds(row, 128), :]

    halves = (
        RingHalf(up_src, x, y, to_x, to_y, u1, u2, uh, oup_ref, sems[:4]),
        RingHalf(down_src, y, x, to_y, to_x, d1, d2, dh, odown_ref, sems[4:]),
    )
    for k in range(4):
        for half in halves:
            half.send_far(k)
    for k in range(4):
        for half in halves:
            half.send_raw(k)
    for k in range(4):
        for half in halves:
            half.pass_on(k)
    for k in range(4):
        for half in halves:
            half.close1(k)
    for half in halves:
        half.pass_on2()
    for half in halves:
        half.close2()
    for half in halves:
        half.finish()


def reduce_grads(up, down):
    dma = pltpu.SemaphoreType.DMA
    return pl.pallas_call(
        reduce_kernel,
        out_shape=(
            jax.ShapeDtypeStruct((2, 512, 128), F32),
            jax.ShapeDtypeStruct((2, 128, 512), F32),
        ),
        in_specs=[pl.BlockSpec(memory_space=pltpu.VMEM)] * 2,
        out_specs=(pl.BlockSpec(memory_space=pltpu.VMEM),) * 2,
        scratch_shapes=[
            pltpu.VMEM((3, 2, 4, 512, 128), BF16),
            pltpu.VMEM((3, 2, 512, 128), BF16),
            pltpu.VMEM((3, 2, 512, 128), BF16),
            pltpu.VMEM((3, 2, 4, 128, 512), BF16),
            pltpu.VMEM((3, 2, 128, 512), BF16),
            pltpu.VMEM((3, 2, 128, 512), BF16),
        ]
        + [dma((3, 2, 4)), dma((3, 2, 4)), dma((3, 2)), dma((3, 2))] * 2,
        compiler_params=pltpu.CompilerParams(
            collective_id=0, has_side_effects=True, vmem_limit_bytes=48 * 1024 * 1024
        ),
        name="reduce_grads",
    )(up, down)


def from_behind(block, axis, distance):
    devices = range(lax.axis_size(axis))
    route = [((i - distance) % len(devices), i) for i in devices]
    return lax.ppermute(block, axis, route)


def layer_norm(values_in):
    mean = jnp.mean(values_in, axis=-1, keepdims=True)
    centred = values_in - mean
    return centred * lax.rsqrt(jnp.mean(centred * centred, axis=-1, keepdims=True) + 1e-05)


def attend(windows, labels, w_qkv, w_proj, logit_scale):
    count, length, width = windows.shape
    heads = logit_scale.shape[0]
    head_dim = width // heads
    normed = layer_norm(windows.astype(jnp.float32)).astype(jnp.bfloat16)
    mixed = jnp.dot(
        normed.reshape(count * length, width), w_qkv, preferred_element_type=jnp.float32
    )
    mixed = mixed.reshape(count, length, 3, heads, head_dim)
    query = mixed[:, :, 0]
    keys = mixed[:, :, 1]
    values = mixed[:, :, 2].astype(jnp.bfloat16)
    query = query / jnp.maximum(jnp.sqrt(jnp.sum(query * query, axis=-1, keepdims=True)), 4.0)
    keys = keys / jnp.maximum(jnp.sqrt(jnp.sum(keys * keys, axis=-1, keepdims=True)), 4.0)
    scores = jnp.einsum("wqhc,wkhc->whqk", query, keys, precision=lax.Precision.HIGHEST)
    scores = scores * logit_scale[None, :, None, None]
    allowed = labels[:, None, :, None] == labels[:, None, None, :]
    weights = jnp.where(allowed, jnp.exp(scores), 0.0)
    probs = (weights / jnp.sum(weights, axis=-1, keepdims=True)).astype(jnp.bfloat16)
    joined = jnp.einsum("whqk,wkhc->wqhc", probs, values, preferred_element_type=jnp.float32)
    joined = joined.astype(jnp.bfloat16).reshape(count * length, width)
    result = jnp.dot(joined, w_proj, preferred_element_type=jnp.float32).astype(jnp.bfloat16)
    return result.reshape(count, length, width)


def expert_grads(rows_in, rows_grad, act, hidden, w_down_part):
    grad_down_e = jnp.einsum(
        "secf,secd->efd", hidden, rows_grad, preferred_element_type=jnp.float32
    )
    grad_hidden = jnp.einsum(
        "secd,efd->secf", rows_grad, w_down_part, preferred_element_type=jnp.float32
    )
    grad_act = jax.vjp(jax.nn.gelu, act)[1](grad_hidden)[0].astype(jnp.bfloat16)
    grad_up_e = jnp.einsum("secd,secf->edf", rows_in, grad_act, preferred_element_type=jnp.float32)
    return (grad_up_e, grad_down_e)


def on_device(tokens, cotangent, w_qkv, w_proj, logit_scale, w_router, w_up, w_down, expert_ids):
    tile = tokens[0]
    rows_t, cols_t, width = tile.shape
    upper = from_behind(tile[rows_t - SHIFT :], "sy", 1)
    row_moved = jnp.concatenate([upper, tile[: rows_t - SHIFT]], 0)
    left = from_behind(row_moved[:, cols_t - SHIFT :], "sx", 1)
    region = jnp.concatenate([left, row_moved[:, : cols_t - SHIFT]], 1)
    row_label = jnp.where((lax.axis_index("sy") == 0) & (jnp.arange(rows_t) >= SHIFT), 1, 0).astype(
        jnp.int32
    )
    col_label = jnp.where((lax.axis_index("sx") == 0) & (jnp.arange(cols_t) >= SHIFT), 1, 0).astype(
        jnp.int32
    )
    label_map = row_label[:, None] * 2 + col_label[None, :]
    rows_h = rows_t // WIN
    cols_w = cols_t // WIN
    length = WIN * WIN
    windows = (
        region.reshape(rows_h, WIN, cols_w, WIN, width)
        .transpose(0, 2, 1, 3, 4)
        .reshape(rows_h * cols_w, length, width)
    )
    labels = (
        label_map.reshape(rows_h, WIN, cols_w, WIN)
        .transpose(0, 2, 1, 3)
        .reshape(rows_h * cols_w, length)
    )
    count_tok = rows_t * cols_t
    experts_all = w_router.shape[1]
    exp_dev = w_up.shape[0]
    n_sx = lax.axis_size("sx")
    cap = 2 * count_tok // experts_all
    slots = experts_all * cap
    ids = expert_ids.reshape(count_tok)
    onehot = ids[:, None] == jnp.arange(experts_all, dtype=jnp.int32)[None, :]
    running = jnp.cumsum(onehot.astype(jnp.int32), axis=0) - 1
    rank = jnp.sum(jnp.where(onehot, running, 0), axis=-1)
    slot = ids * cap + rank
    place = (slot[None, :] == jnp.arange(slots, dtype=jnp.int32)[:, None]).astype(jnp.bfloat16)
    send_cot = jnp.dot(
        place, cotangent[0].reshape(count_tok, width), preferred_element_type=jnp.float32
    ).astype(jnp.bfloat16)
    send_cot = send_cot.reshape(n_sx, exp_dev, cap, width)
    received_cot = lax.all_to_all(send_cot, "sx", split_axis=0, concat_axis=0, tiled=True)
    attended = attend(windows, labels, w_qkv, w_proj, logit_scale)
    attended = (
        attended.reshape(rows_h, cols_w, WIN, WIN, width)
        .transpose(0, 2, 1, 3, 4)
        .reshape(rows_t, cols_t, width)
    )
    right = from_behind(attended[:, :SHIFT], "sx", -1)
    col_home = jnp.concatenate([attended[:, SHIFT:], right], 1)
    lower = from_behind(col_home[:SHIFT], "sy", -1)
    attn_home = jnp.concatenate([col_home[SHIFT:], lower], 0)
    resid = (tile.astype(jnp.float32) + attn_home.astype(jnp.float32)).reshape(count_tok, width)
    normed = layer_norm(resid).astype(jnp.bfloat16)
    logits = jnp.dot(normed, w_router, preferred_element_type=jnp.float32)
    gate = jax.nn.sigmoid(jnp.sum(jnp.where(onehot, logits, 0.0), axis=-1))
    send = jnp.dot(place, normed, preferred_element_type=jnp.float32).astype(jnp.bfloat16)
    send = send.reshape(n_sx, exp_dev, cap, width)
    received = lax.all_to_all(send, "sx", split_axis=0, concat_axis=0, tiled=True)
    act = jnp.einsum("secd,edf->secf", received, w_up, preferred_element_type=jnp.float32)
    hidden = jax.nn.gelu(act).astype(jnp.bfloat16)
    expert_out = jnp.einsum(
        "secf,efd->secd", hidden, w_down, preferred_element_type=jnp.float32
    ).astype(jnp.bfloat16)
    returned = lax.all_to_all(expert_out, "sx", split_axis=0, concat_axis=0, tiled=True)
    moe = jnp.einsum(
        "st,sd->td", place, returned.reshape(slots, width), preferred_element_type=jnp.float32
    )
    mixed = (resid + gate[:, None] * moe).astype(jnp.bfloat16).reshape(1, rows_t, cols_t, width)
    routers = lax.dynamic_slice_in_dim(w_router, lax.axis_index("sx") * exp_dev, exp_dev, 1)
    gates = jnp.einsum("secd,de->sec", received, routers, preferred_element_type=jnp.float32)
    gates = jax.nn.sigmoid(gates)
    received_grad = (gates[..., None] * received_cot.astype(jnp.float32)).astype(jnp.bfloat16)
    full_up, full_down = expert_grads(received, received_grad, act, hidden, w_down)
    grad_up, grad_down = reduce_grads(full_up.astype(jnp.bfloat16), full_down.astype(jnp.bfloat16))
    return (mixed, grad_up, grad_down)


def solution(mesh):
    return jax.shard_map(
        on_device,
        mesh=mesh,
        in_specs=(
            P("dp", "sy", "sx", None),
            P("dp", "sy", "sx", None),
            P(),
            P(),
            P(),
            P(),
            P("sx", None, None),
            P("sx", None, None),
            P("dp", "sy", "sx", None, None),
        ),
        out_specs=(
            P("dp", "sy", "sx", None),
            P("sx", None, ("sy", "dp")),
            P("sx", ("sy", "dp"), None),
        ),
        check_vma=False,
    )
```

```python
import jax
import jax.numpy as jnp
from jax import lax
from jax.experimental import pallas as pl
from jax.experimental.pallas import tpu as pltpu
from jax.sharding import PartitionSpec as P

WIN = 16
SHIFT = 8
MESH = pl.DeviceIdType.MESH
BF16 = jnp.bfloat16
F32 = jnp.float32
N_SX = 16
CAP = 32
NEAR_FIRST = (0, 1, 15, 2, 14, 3, 13, 4, 12, 5, 11, 6, 10, 7, 9, 8)


def dot(a, b):
    return jnp.dot(a, b, preferred_element_type=F32)


def dot_tn(a, b):
    return lax.dot_general(a, b, (((0,), (0,)), ((), ())), preferred_element_type=F32)


def dot_nt(a, b):
    return lax.dot_general(a, b, (((1,), (1,)), ((), ())), preferred_element_type=F32)


def ring_places():
    sy, dp = lax.axis_index("sy"), lax.axis_index("dp")
    y, x = sy // 2, dp * 2 + lax.rem(sy, 2)
    to_x, to_y = [], []
    for step in (1, 3):
        nx, ny = lax.rem(x + step, 4), lax.rem(y + step, 4)
        to_x.append({"sy": y * 2 + lax.rem(nx, 2), "dp": nx // 2})
        to_y.append({"sy": ny * 2 + lax.rem(x, 2)})
    return x, y, to_x, to_y


def shard_of(x, y):
    return y * 4 + lax.rem(x, 2) * 2 + x // 2


def greet(targets):
    barrier = pltpu.get_barrier_semaphore()
    for target in targets:
        pl.semaphore_signal(barrier, inc=1, device_id=target, device_id_type=MESH)
    pl.semaphore_wait(barrier, len(targets))


class RingHalf:
    def __init__(self, block, here_a, here_b, to_a, to_b, stage, bufs1, bufs2, hold, out, sems):
        self.block = block
        self.pa, self.pb = here_a, here_b
        self.to_a, self.to_b = to_a, to_b
        self.stage, self.bufs1, self.bufs2 = stage, bufs1, bufs2
        self.hold = hold
        self.out = out
        self.s1, self.r1, self.s2, self.r2 = sems

    def order(self, k):
        return lax.rem(self.pb + 2 + k + (k // 2) * (1 + 2 * (k % 2)), 4)

    def copy1(self, kind, way, k):
        ref = self.bufs1.at[0, way, k] if kind == 2 else self.stage.at[kind, way, k]
        return pltpu.make_async_remote_copy(
            src_ref=ref,
            dst_ref=self.bufs1.at[kind, way, k],
            send_sem=self.s1.at[kind, way, k],
            recv_sem=self.r1.at[kind, way, k],
            device_id=self.to_a[way],
            device_id_type=MESH,
        )

    def copy2(self, kind, way):
        if kind == 0:
            ref = self.hold.at[0, way]
        elif kind == 1:
            ref = self.hold.at[1, 0] if way == 1 else self.hold.at[2, 1]
        else:
            ref = self.bufs2.at[0, way]
        return pltpu.make_async_remote_copy(
            src_ref=ref,
            dst_ref=self.bufs2.at[kind, way],
            send_sem=self.s2.at[kind, way],
            recv_sem=self.r2.at[kind, way],
            device_id=self.to_b[way],
            device_id_type=MESH,
        )

    def ahead(self, way):
        return lax.rem(self.pa + (1 if way == 0 else 3), 4)

    def send_far(self, k):
        for way in range(2):
            part = self.block(way, lax.rem(self.pa + 2, 4), self.order(k))
            self.stage[0, way, k] = part.astype(BF16)
            self.copy1(0, way, k).start()

    def send_raw(self, k):
        for way in range(2):
            part = self.block(1 - way, self.ahead(way), self.order(k))
            self.stage[1, way, k] = part.astype(BF16)
            self.copy1(1, way, k).start()

    def pass_on(self, k):
        for way in range(2):
            mine = self.block(way, self.ahead(way), self.order(k))
            self.copy1(0, way, k).wait_recv()
            self.bufs1[0, way, k] = (self.bufs1[0, way, k].astype(F32) + mine).astype(BF16)
            self.copy1(2, way, k).start()

    def close1(self, k):
        for e in range(2):
            total = self.block(e, self.pa, self.order(k))
            self.copy1(1, 1 - e, k).wait_recv()
            self.copy1(2, e, k).wait_recv()
            total = total + self.bufs1[1, 1 - e, k].astype(F32)
            total = total + self.bufs1[2, e, k].astype(F32)
            if k < 3:
                self.hold[k, e] = total.astype(BF16)
            else:
                self.out[e] = total
        if k == 0:
            self.copy2(0, 0).start()
            self.copy2(0, 1).start()
        elif k == 1:
            self.copy2(1, 1).start()
        elif k == 2:
            self.copy2(1, 0).start()

    def pass_on2(self):
        for way in range(2):
            self.copy2(0, way).wait_recv()
            mine = self.hold[2 - way, way].astype(F32)
            self.bufs2[0, way] = (self.bufs2[0, way].astype(F32) + mine).astype(BF16)
            self.copy2(2, way).start()

    def close2(self):
        for e in range(2):
            self.copy2(1, 1 - e).wait_recv()
            self.copy2(2, e).wait_recv()
            total = self.out[e] + self.bufs2[1, 1 - e].astype(F32)
            self.out[e] = total + self.bufs2[2, e].astype(F32)

    def finish(self):
        for kind in range(3):
            for way in range(2):
                for k in range(4):
                    self.copy1(kind, way, k).wait_send()
                self.copy2(kind, way).wait_send()


class Exchange:
    def __init__(self, me, away, source, landing, send_sem, recv_sem):
        self.me, self.away = me, away
        self.source, self.landing = source, landing
        self.send_sem, self.recv_sem = send_sem, recv_sem

    def peer(self, slot):
        d = NEAR_FIRST[slot]
        return lax.rem(self.me + (d if self.away else N_SX - d), N_SX)

    def copy(self, slot):
        peer = self.peer(slot)
        return pltpu.make_async_remote_copy(
            src_ref=self.source(slot, peer),
            dst_ref=self.landing(slot, self.me),
            send_sem=self.send_sem.at[slot],
            recv_sem=self.recv_sem.at[slot],
            device_id={"sx": peer},
            device_id_type=MESH,
        )


def gelu_parts(v):
    c = 0.7978845608028654
    sq = v * v
    t = jnp.tanh(c * v * (1.0 + 0.044715 * sq))
    half = 0.5 + 0.5 * t
    slope = half + (0.5 * c) * v * (1.0 - t * t) * (1.0 + (3 * 0.044715) * sq)
    return v * half, slope


def moe_kernel(
    send_ref, cot_ref, place_ref, resid_ref, gate_ref, router_ref, wup_any, wdown_any,
    mixed_ref, oup_ref, odown_ref,
    wup, wdown, recv, cotr, rgrad, rows_t, hidden, gact, rout, back,
    us, u1, u2, uh, ds, d1, d2, dh,
    wsem, lsem, xs, xr, cs, cr, bs, br, *sems,
):
    me = lax.axis_index("sx")
    x, y, to_x, to_y = ring_places()
    loads = []
    for e in range(2):
        loads.append(pltpu.make_async_copy(wup_any.at[e], wup.at[e], wsem.at[0, e]))
        loads.append(pltpu.make_async_copy(wdown_any.at[e], wdown.at[e], wsem.at[1, e]))
    for load in loads:
        load.start()
    rows_out = Exchange(
        me, True, lambda s, p: send_ref.at[p], lambda s, m: recv.at[:, s], xs, xr
    )
    cots_out = Exchange(
        me, True, lambda s, p: cot_ref.at[p], lambda s, m: cotr.at[:, s], cs, cr
    )
    home = Exchange(me, False, lambda s, p: rout.at[s], lambda s, m: back.at[m], bs, br)
    greet([{"sx": rows_out.peer(s)} for s in range(1, N_SX)] + to_x + to_y)
    for s in range(1, N_SX):
        rows_out.copy(s).start()
    for s in range(1, N_SX):
        cots_out.copy(s).start()
    recv[:, 0] = send_ref[me]
    cotr[:, 0] = cot_ref[me]
    for load in loads:
        load.wait()

    def hidden_part(g):
        for s in range(max(1, 8 * g), 8 * g + 8):
            rows_out.copy(s).wait_recv()
            cots_out.copy(s).wait_recv()
        for e in range(2):
            rows = recv[e, 8 * g : 8 * g + 8].reshape(256, 512)
            cot = cotr[e, 8 * g : 8 * g + 8].reshape(256, 512)
            logits = dot(rows, router_ref[...])
            column = lax.broadcasted_iota(jnp.int32, logits.shape, 1) == 2 * me + e
            gate = jax.nn.sigmoid(jnp.sum(jnp.where(column, logits, 0.0), axis=1, keepdims=True))
            grad = (gate * cot.astype(F32)).astype(BF16)
            rgrad[e, 256 * g : 256 * g + 256] = grad
            rows_t[e, :, 256 * g : 256 * g + 256] = rows.T

            def step(f, carry):
                part = pl.ds(pl.multiple_of(f * 512, 512), 512)
                act = dot(rows, wup[e, :, part])
                hid, slope = gelu_parts(act)
                hidden[e, 256 * g : 256 * g + 256, part] = hid.astype(BF16)
                through = dot_nt(grad, wdown[e, part, :])
                gact[e, 256 * g : 256 * g + 256, part] = (through * slope).astype(BF16)
                return carry

            lax.fori_loop(0, 4, step, 0)

    def return_part(g):
        for e in range(2):
            out = dot(hidden[e, 256 * g : 256 * g + 256], wdown[e]).astype(BF16)
            rout[8 * g : 8 * g + 8, e] = out.reshape(8, CAP, 512)
        for s in range(8 * g, 8 * g + 8):
            if s:
                home.copy(s).start()
        if g == 0:
            back[me] = rout[0]

    def up_block(e, ix, iy):
        col = pl.multiple_of(shard_of(ix, iy) * 128, 128)
        return dot(rows_t[e], gact[e, :, pl.ds(col, 128)])

    def down_block(e, iy, ix):
        col = pl.multiple_of(shard_of(ix, iy) * 128, 128)
        return dot_tn(hidden[e, :, pl.ds(col, 128)], rgrad[e])

    halves = (
        RingHalf(up_block, x, y, to_x, to_y, us, u1, u2, uh, oup_ref, sems[:4]),
        RingHalf(down_block, y, x, to_y, to_x, ds, d1, d2, dh, odown_ref, sems[4:]),
    )

    def each(method):
        def step(k, carry):
            for half in halves:
                getattr(half, method)(k)
            return carry

        lax.fori_loop(0, 4, step, 0)

    hidden_part(0)
    return_part(0)
    hidden_part(1)
    each("send_far")
    return_part(1)
    each("send_raw")
    each("pass_on")
    for k in range(4):
        for half in halves:
            half.close1(k)
    for half in halves:
        half.pass_on2()
    for s in range(1, N_SX):
        home.copy(s).wait_recv()
    moe = dot_tn(place_ref[...], back[...].reshape(1024, 512))
    mixed_ref[...] = (resid_ref[...] + gate_ref[...] * moe).astype(BF16)
    for half in halves:
        half.close2()
    for half in halves:
        half.finish()
    for s in range(1, N_SX):
        rows_out.copy(s).wait_send()
        cots_out.copy(s).wait_send()
        home.copy(s).wait_send()


def expert_layer(send, send_cot, place, resid, gate, w_router, w_up, w_down):
    dma = pltpu.SemaphoreType.DMA
    vmem = pl.BlockSpec(memory_space=pltpu.VMEM)
    anywhere = pl.BlockSpec(memory_space=pl.ANY)
    ring = [dma((3, 2, 4)), dma((3, 2, 4)), dma((3, 2)), dma((3, 2))]
    return pl.pallas_call(
        moe_kernel,
        out_shape=(
            jax.ShapeDtypeStruct((512, 512), BF16),
            jax.ShapeDtypeStruct((2, 512, 128), F32),
            jax.ShapeDtypeStruct((2, 128, 512), F32),
        ),
        in_specs=[vmem] * 6 + [anywhere] * 2,
        out_specs=(vmem,) * 3,
        scratch_shapes=[
            pltpu.VMEM((2, 512, 2048), BF16),
            pltpu.VMEM((2, 2048, 512), BF16),
            pltpu.VMEM((2, N_SX, CAP, 512), BF16),
            pltpu.VMEM((2, N_SX, CAP, 512), BF16),
            pltpu.VMEM((2, 512, 512), BF16),
            pltpu.VMEM((2, 512, 512), BF16),
            pltpu.VMEM((2, 512, 2048), BF16),
            pltpu.VMEM((2, 512, 2048), BF16),
            pltpu.VMEM((N_SX, 2, CAP, 512), BF16),
            pltpu.VMEM((N_SX, 2, CAP, 512), BF16),
            pltpu.VMEM((2, 2, 4, 512, 128), BF16),
            pltpu.VMEM((3, 2, 4, 512, 128), BF16),
            pltpu.VMEM((3, 2, 512, 128), BF16),
            pltpu.VMEM((3, 2, 512, 128), BF16),
            pltpu.VMEM((2, 2, 4, 128, 512), BF16),
            pltpu.VMEM((3, 2, 4, 128, 512), BF16),
            pltpu.VMEM((3, 2, 128, 512), BF16),
            pltpu.VMEM((3, 2, 128, 512), BF16),
            dma((2, 2)),
            dma((2,)),
        ]
        + [dma((N_SX,))] * 6
        + ring * 2,
        compiler_params=pltpu.CompilerParams(
            collective_id=0, has_side_effects=True, vmem_limit_bytes=56 * 1024 * 1024
        ),
        name="expert_layer",
    )(send, send_cot, place, resid, gate, w_router, w_up, w_down)


def from_behind(block, axis, distance):
    devices = range(lax.axis_size(axis))
    route = [((i - distance) % len(devices), i) for i in devices]
    return lax.ppermute(block, axis, route)


def layer_norm(values_in):
    mean = jnp.mean(values_in, axis=-1, keepdims=True)
    centred = values_in - mean
    return centred * lax.rsqrt(jnp.mean(centred * centred, axis=-1, keepdims=True) + 1e-05)


def attend(windows, labels, w_qkv, w_proj, logit_scale):
    count, length, width = windows.shape
    heads = logit_scale.shape[0]
    head_dim = width // heads
    normed = layer_norm(windows.astype(jnp.float32)).astype(jnp.bfloat16)
    mixed = jnp.dot(
        normed.reshape(count * length, width), w_qkv, preferred_element_type=jnp.float32
    )
    mixed = mixed.reshape(count, length, 3, heads, head_dim)
    query = mixed[:, :, 0]
    keys = mixed[:, :, 1]
    values = mixed[:, :, 2].astype(jnp.bfloat16)
    query = query / jnp.maximum(jnp.sqrt(jnp.sum(query * query, axis=-1, keepdims=True)), 4.0)
    keys = keys / jnp.maximum(jnp.sqrt(jnp.sum(keys * keys, axis=-1, keepdims=True)), 4.0)
    scores = jnp.einsum("wqhc,wkhc->whqk", query, keys, precision=lax.Precision.HIGHEST)
    scores = scores * logit_scale[None, :, None, None]
    allowed = labels[:, None, :, None] == labels[:, None, None, :]
    weights = jnp.where(allowed, jnp.exp(scores), 0.0)
    probs = (weights / jnp.sum(weights, axis=-1, keepdims=True)).astype(jnp.bfloat16)
    joined = jnp.einsum("whqk,wkhc->wqhc", probs, values, preferred_element_type=jnp.float32)
    joined = joined.astype(jnp.bfloat16).reshape(count * length, width)
    result = jnp.dot(joined, w_proj, preferred_element_type=jnp.float32).astype(jnp.bfloat16)
    return result.reshape(count, length, width)


def on_device(tokens, cotangent, w_qkv, w_proj, logit_scale, w_router, w_up, w_down, expert_ids):
    tile = tokens[0]
    rows_t, cols_t, width = tile.shape
    upper = from_behind(tile[rows_t - SHIFT :], "sy", 1)
    row_moved = jnp.concatenate([upper, tile[: rows_t - SHIFT]], 0)
    left = from_behind(row_moved[:, cols_t - SHIFT :], "sx", 1)
    region = jnp.concatenate([left, row_moved[:, : cols_t - SHIFT]], 1)
    row_label = jnp.where((lax.axis_index("sy") == 0) & (jnp.arange(rows_t) >= SHIFT), 1, 0).astype(
        jnp.int32
    )
    col_label = jnp.where((lax.axis_index("sx") == 0) & (jnp.arange(cols_t) >= SHIFT), 1, 0).astype(
        jnp.int32
    )
    label_map = row_label[:, None] * 2 + col_label[None, :]
    rows_h = rows_t // WIN
    cols_w = cols_t // WIN
    length = WIN * WIN
    windows = (
        region.reshape(rows_h, WIN, cols_w, WIN, width)
        .transpose(0, 2, 1, 3, 4)
        .reshape(rows_h * cols_w, length, width)
    )
    labels = (
        label_map.reshape(rows_h, WIN, cols_w, WIN)
        .transpose(0, 2, 1, 3)
        .reshape(rows_h * cols_w, length)
    )
    count_tok = rows_t * cols_t
    experts_all = w_router.shape[1]
    exp_dev = w_up.shape[0]
    n_sx = lax.axis_size("sx")
    cap = 2 * count_tok // experts_all
    slots = experts_all * cap
    ids = expert_ids.reshape(count_tok)
    onehot = ids[:, None] == jnp.arange(experts_all, dtype=jnp.int32)[None, :]
    running = jnp.cumsum(onehot.astype(jnp.int32), axis=0) - 1
    rank = jnp.sum(jnp.where(onehot, running, 0), axis=-1)
    slot = ids * cap + rank
    place = (slot[None, :] == jnp.arange(slots, dtype=jnp.int32)[:, None]).astype(jnp.bfloat16)
    send_cot = jnp.dot(
        place, cotangent[0].reshape(count_tok, width), preferred_element_type=jnp.float32
    ).astype(jnp.bfloat16)
    send_cot = send_cot.reshape(n_sx, exp_dev, cap, width)
    attended = attend(windows, labels, w_qkv, w_proj, logit_scale)
    attended = (
        attended.reshape(rows_h, cols_w, WIN, WIN, width)
        .transpose(0, 2, 1, 3, 4)
        .reshape(rows_t, cols_t, width)
    )
    right = from_behind(attended[:, :SHIFT], "sx", -1)
    col_home = jnp.concatenate([attended[:, SHIFT:], right], 1)
    lower = from_behind(col_home[:SHIFT], "sy", -1)
    attn_home = jnp.concatenate([col_home[SHIFT:], lower], 0)
    resid = (tile.astype(jnp.float32) + attn_home.astype(jnp.float32)).reshape(count_tok, width)
    normed = layer_norm(resid).astype(jnp.bfloat16)
    logits = jnp.dot(normed, w_router, preferred_element_type=jnp.float32)
    gate = jax.nn.sigmoid(jnp.sum(jnp.where(onehot, logits, 0.0), axis=-1))
    send = jnp.dot(place, normed, preferred_element_type=jnp.float32).astype(jnp.bfloat16)
    send = send.reshape(n_sx, exp_dev, cap, width)
    mixed, grad_up, grad_down = expert_layer(
        send, send_cot, place, resid, gate[:, None], w_router, w_up, w_down
    )
    mixed = mixed.reshape(1, rows_t, cols_t, width)
    return (mixed, grad_up, grad_down)


def solution(mesh):
    return jax.shard_map(
        on_device,
        mesh=mesh,
        in_specs=(
            P("dp", "sy", "sx", None),
            P("dp", "sy", "sx", None),
            P(),
            P(),
            P(),
            P(),
            P("sx", None, None),
            P("sx", None, None),
            P("dp", "sy", "sx", None, None),
        ),
        out_specs=(
            P("dp", "sy", "sx", None),
            P("sx", None, ("sy", "dp")),
            P("sx", ("sy", "dp"), None),
        ),
        check_vma=False,
    )
```

```python
import jax
import jax.numpy as jnp
from jax import lax
from jax.experimental import pallas as pl
from jax.experimental.pallas import tpu as pltpu
from jax.sharding import PartitionSpec as P

MESH = pl.DeviceIdType.MESH
BF16 = jnp.bfloat16
F32 = jnp.float32
N_SX = 16
VMEM_MIB = 52
CAP = 32
NEAR_FIRST = (0, 1, 15, 2, 14, 3, 13, 4, 12, 5, 11, 6, 10, 7, 9, 8)


def dot(a, b):
    return jnp.dot(a, b, preferred_element_type=F32)


def dot_tn(a, b):
    return lax.dot_general(a, b, (((0,), (0,)), ((), ())), preferred_element_type=F32)


def dot_nt(a, b):
    return lax.dot_general(a, b, (((1,), (1,)), ((), ())), preferred_element_type=F32)


def ring_places():
    sy, dp = lax.axis_index("sy"), lax.axis_index("dp")
    y, x = sy // 2, dp * 2 + lax.rem(sy, 2)
    to_x, to_y = [], []
    for step in (1, 3):
        nx, ny = lax.rem(x + step, 4), lax.rem(y + step, 4)
        to_x.append({"sy": y * 2 + lax.rem(nx, 2), "dp": nx // 2})
        to_y.append({"sy": ny * 2 + lax.rem(x, 2)})
    return x, y, to_x, to_y


def shard_of(x, y):
    return y * 4 + lax.rem(x, 2) * 2 + x // 2


class RingHalf:
    def __init__(self, block, here_a, here_b, to_a, to_b, stage, bufs1, bufs2, hold, out, sems):
        self.block = block
        self.pa, self.pb = here_a, here_b
        self.to_a, self.to_b = to_a, to_b
        self.stage, self.bufs1, self.bufs2 = stage, bufs1, bufs2
        self.hold = hold
        self.out = out
        self.s1, self.r1, self.s2, self.r2 = sems

    def order(self, k):
        return lax.rem(self.pb + 2 + k + (k // 2) * (1 + 2 * (k % 2)), 4)

    def copy1(self, kind, way, k):
        ref = self.bufs1.at[0, way, k] if kind == 2 else self.stage.at[kind, way, k]
        return pltpu.make_async_remote_copy(
            src_ref=ref,
            dst_ref=self.bufs1.at[kind, way, k],
            send_sem=self.s1.at[kind, way, k],
            recv_sem=self.r1.at[kind, way, k],
            device_id=self.to_a[way],
            device_id_type=MESH,
        )

    def copy2(self, kind, way):
        if kind == 0:
            ref = self.hold.at[0, way]
        elif kind == 1:
            ref = self.hold.at[1, 0] if way == 1 else self.hold.at[2, 1]
        else:
            ref = self.bufs2.at[0, way]
        return pltpu.make_async_remote_copy(
            src_ref=ref,
            dst_ref=self.bufs2.at[kind, way],
            send_sem=self.s2.at[kind, way],
            recv_sem=self.r2.at[kind, way],
            device_id=self.to_b[way],
            device_id_type=MESH,
        )

    def ahead(self, way):
        return lax.rem(self.pa + (1 if way == 0 else 3), 4)

    def send_far(self, k):
        for way in range(2):
            part = self.block(way, lax.rem(self.pa + 2, 4), self.order(k))
            self.stage[0, way, k] = part.astype(BF16)
            self.copy1(0, way, k).start()

    def send_raw(self, k):
        for way in range(2):
            part = self.block(1 - way, self.ahead(way), self.order(k))
            self.stage[1, way, k] = part.astype(BF16)
            self.copy1(1, way, k).start()

    def pass_on(self, k):
        for way in range(2):
            mine = self.block(way, self.ahead(way), self.order(k))
            self.copy1(0, way, k).wait_recv()
            self.bufs1[0, way, k] = (self.bufs1[0, way, k].astype(F32) + mine).astype(BF16)
            self.copy1(2, way, k).start()

    def close1(self, k):
        for e in range(2):
            total = self.block(e, self.pa, self.order(k))
            self.copy1(1, 1 - e, k).wait_recv()
            self.copy1(2, e, k).wait_recv()
            total = total + self.bufs1[1, 1 - e, k].astype(F32)
            total = total + self.bufs1[2, e, k].astype(F32)
            if k < 3:
                self.hold[k, e] = total.astype(BF16)
            else:
                self.out[e] = total
        if k == 0:
            self.copy2(0, 0).start()
            self.copy2(0, 1).start()
        elif k == 1:
            self.copy2(1, 1).start()
        elif k == 2:
            self.copy2(1, 0).start()

    def pass_on2(self):
        for way in range(2):
            self.copy2(0, way).wait_recv()
            mine = self.hold[2 - way, way].astype(F32)
            self.bufs2[0, way] = (self.bufs2[0, way].astype(F32) + mine).astype(BF16)
            self.copy2(2, way).start()

    def close2(self):
        for e in range(2):
            self.copy2(1, 1 - e).wait_recv()
            self.copy2(2, e).wait_recv()
            total = self.out[e] + self.bufs2[1, 1 - e].astype(F32)
            self.out[e] = total + self.bufs2[2, e].astype(F32)

    def finish(self):
        for kind in range(3):
            for way in range(2):
                for k in range(4):
                    self.copy1(kind, way, k).wait_send()
                self.copy2(kind, way).wait_send()


class Exchange:
    def __init__(self, me, away, source, landing, send_sem, recv_sem):
        self.me, self.away = me, away
        self.source, self.landing = source, landing
        self.send_sem, self.recv_sem = send_sem, recv_sem

    def peer(self, slot):
        d = NEAR_FIRST[slot]
        return lax.rem(self.me + (d if self.away else N_SX - d), N_SX)

    def copy(self, slot):
        peer = self.peer(slot)
        return pltpu.make_async_remote_copy(
            src_ref=self.source(slot, peer),
            dst_ref=self.landing(slot, self.me),
            send_sem=self.send_sem.at[slot],
            recv_sem=self.recv_sem.at[slot],
            device_id={"sx": peer},
            device_id_type=MESH,
        )


def gelu_parts(v):
    c = 0.7978845608028654
    sq = v * v
    t = jnp.tanh(c * v * (1.0 + 0.044715 * sq))
    half = 0.5 + 0.5 * t
    slope = half + (0.5 * c) * v * (1.0 - t * t) * (1.0 + (3 * 0.044715) * sq)
    return v * half, slope


def layer_norm(v):
    centred = v - jnp.mean(v, axis=-1, keepdims=True)
    return centred * lax.rsqrt(jnp.mean(centred * centred, axis=-1, keepdims=True) + 1e-05)


def split(v):
    high = v.astype(BF16)
    return high, (v - high.astype(F32)).astype(BF16)


def head_inverse(v, ones):
    high, low = split(v * v)
    total = dot(jnp.concatenate([high, low], axis=1), ones)
    return jnp.minimum(lax.rsqrt(total), 0.25)


def attend_group(qkv, joined, g, scale_ref, ones, same):
    part = [pl.ds(pl.multiple_of(n * 512 + g * 128, 128), 128) for n in range(3)]
    query, key, value = [qkv[:, p] for p in part]
    query = query * (head_inverse(query, ones) * scale_ref[:, part[0]])
    k_high, k_low = split(key * head_inverse(key, ones))
    keys = jnp.concatenate([k_high, k_high, k_low], axis=1)
    value = value.astype(BF16)
    values = jnp.concatenate([value, jnp.ones_like(value)], axis=1)
    head = lax.shift_right_logical(lax.broadcasted_iota(jnp.int32, query.shape, 1), 5)
    top, bottom = jnp.zeros_like(query), jnp.ones_like(query)
    for i in range(4):
        q_high, q_low = split(jnp.where(head == i, query, 0.0))
        scores = dot_nt(jnp.concatenate([q_high, q_low, q_high], axis=1), keys)
        weights = (jnp.exp(scores) * same).astype(BF16)
        out = dot(weights, values)
        top = jnp.where(head == i, out[:, :128], top)
        bottom = jnp.where(head == i, out[:, 128:], bottom)
    joined[:, part[0]] = (top / bottom).astype(BF16)


def block_kernel(
    tok_ref, cot_ref, ids_ref, scale_ref, router_ref, wqkv_any, wproj_any, wup_any, wdown_any,
    mixed_ref, oup_ref, odown_ref,
    wqkv, wproj, wup, wdown,
    resid, nsend, region, qkv, joined, attb, homeb, place, place_t, normed2, gate_s,
    send, csend, recv, cotr, rgrad, rows_t, hidden, gact, back,
    us, u1, u2, uh, ds, d1, d2, dh,
    wsem, hs, hr, ks, kr, xs, xr, cs, cr, bs, br, *sems,
):
    me, sy = lax.axis_index("sx"), lax.axis_index("sy")
    n_sy = lax.axis_size("sy")
    x, y, to_x, to_y = ring_places()
    rows_out = Exchange(me, True, lambda s, p: send.at[p], lambda s, m: recv.at[:, s], xs, xr)
    cots_out = Exchange(me, True, lambda s, p: csend.at[p], lambda s, m: cotr.at[:, s], cs, cr)
    home = Exchange(me, False, lambda s, p: csend.at[s], lambda s, m: back.at[m], bs, br)
    below, above = lax.rem(sy + 1, n_sy), lax.rem(sy + n_sy - 1, n_sy)
    after, before = lax.rem(me + 1, N_SX), lax.rem(me + N_SX - 1, N_SX)
    onward = [{"sy": below}] * 3 + [{"sx": after}, {"sy": below, "sx": after}]
    backward = [{"sy": above}] * 3 + [{"sx": before}, {"sy": above, "sx": before}]
    greeted = [{"sx": rows_out.peer(s)} for s in range(1, N_SX)] + to_x + to_y
    greeted += [onward[0], onward[4], backward[0], backward[4]]
    barrier = pltpu.get_barrier_semaphore()
    for target in greeted:
        pl.semaphore_signal(barrier, inc=1, device_id=target, device_id_type=MESH)

    loads = [
        pltpu.make_async_copy(wqkv_any, wqkv, wsem.at[0]),
        pltpu.make_async_copy(wproj_any, wproj, wsem.at[1]),
        pltpu.make_async_copy(wup_any, wup, wsem.at[2]),
        pltpu.make_async_copy(wdown_any, wdown, wsem.at[3]),
    ]
    for load in loads:
        load.start()

    places = ((1, 0), (2, 0), (3, 0), (0, 1), (0, 0))

    def tile_at(cg, rh):
        return (slice(8 * rh, 8 * rh + 8), slice(8 * cg, 8 * cg + 8))

    resid[...] = tok_ref[...].astype(F32)
    for piece, (cg, rh) in enumerate(places):
        from_cg, from_rh = (cg + 3) % 4, 1 - rh
        block = layer_norm(resid[tile_at(from_cg, from_rh)].reshape(64, 512))
        nsend[piece] = block.astype(BF16)
    for cg in range(1, 4):
        block = layer_norm(resid[tile_at(cg - 1, 0)].reshape(64, 512))
        region[cg, 1] = block.astype(BF16)

    def halo(piece, forward):
        cg, rh = places[piece]
        return pltpu.make_async_remote_copy(
            src_ref=nsend.at[piece] if forward else attb.at[cg, rh],
            dst_ref=region.at[cg, rh] if forward else homeb.at[piece],
            send_sem=(hs if forward else ks).at[piece],
            recv_sem=(hr if forward else kr).at[piece],
            device_id=(onward if forward else backward)[piece],
            device_id_type=MESH,
        )

    pl.semaphore_wait(barrier, len(greeted))
    for piece in (1, 2, 0, 4, 3):
        halo(piece, True).start()

    ids = ids_ref[...]
    named = lax.broadcasted_iota(jnp.int32, (512, 32), 1) == ids
    earlier = lax.broadcasted_iota(jnp.int32, (512, 512), 0) > lax.broadcasted_iota(
        jnp.int32, (512, 512), 1
    )
    counts = dot(jnp.where(earlier, 1.0, 0.0).astype(BF16), jnp.where(named, 1.0, 0.0).astype(BF16))
    rank = jnp.sum(jnp.where(named, counts, 0.0), axis=1, keepdims=True)
    slot = ids.astype(F32) * float(CAP) + rank
    for c in range(4):
        here = (lax.broadcasted_iota(jnp.int32, (512, 256), 1) + 256 * c).astype(F32)
        picked = jnp.where(here == slot, 1.0, 0.0).astype(BF16)
        place_t[:, 256 * c : 256 * c + 256] = picked
        place[256 * c : 256 * c + 256] = picked.T

    def gather(c, rows_ref, out_ref):
        rows = dot(place[256 * c : 256 * c + 256], rows_ref[...]).astype(BF16)
        out_ref[4 * c : 4 * c + 4] = rows.reshape(4, 2, CAP, 512)

    for c in range(4):
        gather(c, cot_ref, csend)
    for s in range(1, N_SX):
        cots_out.copy(s).start()
    cotr[:, 0] = csend[me]

    lane = lax.shift_right_logical(lax.broadcasted_iota(jnp.int32, (256, 128), 1), 5)
    row = lax.shift_right_logical(
        jnp.bitwise_and(lax.broadcasted_iota(jnp.int32, (256, 128), 0), 127), 5
    )
    ones = jnp.where(lane == row, 1.0, 0.0).astype(BF16)

    loads[0].wait()
    loads[1].wait()
    row_cut = jnp.where(sy == 0, 1, 0)
    for w in (1, 0):
        for piece in (1, 2) if w else (0, 4, 3):
            halo(piece, True).wait_recv()
        qkv[...] = dot(region[2 * w : 2 * w + 2].reshape(256, 512), wqkv[...])
        col_cut = jnp.where(me == 0, 1 - w, 0)

        def label(axis):
            b = lax.shift_right_logical(lax.broadcasted_iota(jnp.int32, (256, 256), axis), 6)
            return jnp.bitwise_and(b, 1) * (2 * row_cut) + lax.shift_right_logical(b, 1) * col_cut

        same = jnp.where(label(0) == label(1), 1.0, 0.0)

        def group(g, carry):
            attend_group(qkv, joined, g, scale_ref, ones, same)
            return carry

        lax.fori_loop(0, 4, group, 0)
        attended = dot(joined[...], wproj[...]).astype(BF16)
        attb[2 * w : 2 * w + 2] = attended.reshape(2, 2, 64, 512)
        for piece in (1, 2) if w else (0, 4, 3):
            halo(piece, False).start()
        for cg in (2, 3) if w else (1,):
            resid[tile_at(cg - 1, 0)] += attb[cg, 1].astype(F32).reshape(8, 8, 512)
    for piece in (1, 2, 0, 4, 3):
        cg, rh = places[piece]
        halo(piece, False).wait_recv()
        at = tile_at((cg + 3) % 4, 1 - rh)
        resid[at] += homeb[piece].astype(F32).reshape(8, 8, 512)
    for c in range(4):
        rows = layer_norm(resid[4 * c : 4 * c + 4].reshape(128, 512))
        normed2[128 * c : 128 * c + 128] = rows.astype(BF16)
    for c in range(4):
        gather(c, normed2, send)
    for s in range(1, N_SX):
        rows_out.copy(s).start()
    recv[:, 0] = send[me]
    logits = dot(normed2[...], router_ref[...])
    gate_s[...] = jax.nn.sigmoid(jnp.sum(jnp.where(named, logits, 0.0), axis=1, keepdims=True))
    loads[2].wait()
    loads[3].wait()
    for s in range(1, N_SX):
        cots_out.copy(s).wait_send()
    def hidden_part(g):
        for s in range(max(1, 8 * g), 8 * g + 8):
            rows_out.copy(s).wait_recv()
            cots_out.copy(s).wait_recv()
        for e in range(2):
            rows = recv[e, 8 * g : 8 * g + 8].reshape(256, 512)
            cot = cotr[e, 8 * g : 8 * g + 8].reshape(256, 512)
            logits = dot(rows, router_ref[...])
            column = lax.broadcasted_iota(jnp.int32, logits.shape, 1) == 2 * me + e
            gate = jax.nn.sigmoid(jnp.sum(jnp.where(column, logits, 0.0), axis=1, keepdims=True))
            grad = (gate * cot.astype(F32)).astype(BF16)
            rgrad[e, 256 * g : 256 * g + 256] = grad
            rows_t[e, :, 256 * g : 256 * g + 256] = rows.T

            def step(f, carry):
                part = pl.ds(pl.multiple_of(f * 512, 512), 512)
                act = dot(rows, wup[e, :, part])
                hid, slope = gelu_parts(act)
                hidden[e, 256 * g : 256 * g + 256, part] = hid.astype(BF16)
                through = dot_nt(grad, wdown[e, part, :])
                gact[e, 256 * g : 256 * g + 256, part] = (through * slope).astype(BF16)
                return carry

            lax.fori_loop(0, 4, step, 0)

    def return_part(g):
        for e in range(2):
            out = dot(hidden[e, 256 * g : 256 * g + 256], wdown[e]).astype(BF16)
            csend[8 * g : 8 * g + 8, e] = out.reshape(8, CAP, 512)
        for s in range(8 * g, 8 * g + 8):
            if s:
                home.copy(s).start()
        if g == 0:
            back[me] = csend[0]

    def up_block(e, ix, iy):
        col = pl.multiple_of(shard_of(ix, iy) * 128, 128)
        return dot(rows_t[e], gact[e, :, pl.ds(col, 128)])

    def down_block(e, iy, ix):
        col = pl.multiple_of(shard_of(ix, iy) * 128, 128)
        return dot_tn(hidden[e, :, pl.ds(col, 128)], rgrad[e])

    halves = (
        RingHalf(up_block, x, y, to_x, to_y, us, u1, u2, uh, oup_ref, sems[:4]),
        RingHalf(down_block, y, x, to_y, to_x, ds, d1, d2, dh, odown_ref, sems[4:]),
    )

    def each(method):
        def step(k, carry):
            for half in halves:
                getattr(half, method)(k)
            return carry

        lax.fori_loop(0, 4, step, 0)

    hidden_part(0)
    return_part(0)
    hidden_part(1)
    each("send_far")
    return_part(1)
    each("send_raw")
    each("pass_on")
    for k in range(4):
        for half in halves:
            half.close1(k)
    for half in halves:
        half.pass_on2()
    for s in range(1, N_SX):
        home.copy(s).wait_recv()
    moe = dot(place_t[...], back[...].reshape(1024, 512))
    mixed_ref[...] = (resid[...].reshape(512, 512) + gate_s[...] * moe).astype(BF16)
    for half in halves:
        half.close2()
    for half in halves:
        half.finish()
    for s in range(1, N_SX):
        rows_out.copy(s).wait_send()
        home.copy(s).wait_send()
    for piece in range(5):
        halo(piece, True).wait_send()
        halo(piece, False).wait_send()


def on_device(tokens, cotangent, w_qkv, w_proj, logit_scale, w_router, w_up, w_down, expert_ids):
    dma = pltpu.SemaphoreType.DMA
    vmem = pl.BlockSpec(memory_space=pltpu.VMEM)
    anywhere = pl.BlockSpec(memory_space=pl.ANY)
    ring = [dma((3, 2, 4)), dma((3, 2, 4)), dma((3, 2)), dma((3, 2))]
    buffers = [
        ((512, 1536), BF16),
        ((512, 512), BF16),
        ((2, 512, 2048), BF16),
        ((2, 2048, 512), BF16),
        ((16, 32, 512), F32),
        ((5, 64, 512), BF16),
        ((4, 2, 64, 512), BF16),
        ((256, 1536), F32),
        ((256, 512), BF16),
        ((4, 2, 64, 512), BF16),
        ((5, 64, 512), BF16),
        ((1024, 512), BF16),
        ((512, 1024), BF16),
        ((512, 512), BF16),
        ((512, 1), F32),
        ((N_SX, 2, CAP, 512), BF16),
        ((N_SX, 2, CAP, 512), BF16),
        ((2, N_SX, CAP, 512), BF16),
        ((2, N_SX, CAP, 512), BF16),
        ((2, 512, 512), BF16),
        ((2, 512, 512), BF16),
        ((2, 512, 2048), BF16),
        ((2, 512, 2048), BF16),
        ((N_SX, 2, CAP, 512), BF16),
        ((2, 2, 4, 512, 128), BF16),
        ((3, 2, 4, 512, 128), BF16),
        ((3, 2, 512, 128), BF16),
        ((3, 2, 512, 128), BF16),
        ((2, 2, 4, 128, 512), BF16),
        ((3, 2, 4, 128, 512), BF16),
        ((3, 2, 128, 512), BF16),
        ((3, 2, 128, 512), BF16),
    ]
    scale = jnp.repeat(logit_scale, 32)[None, :]
    mixed, grad_up, grad_down = pl.pallas_call(
        block_kernel,
        out_shape=(
            jax.ShapeDtypeStruct((512, 512), BF16),
            jax.ShapeDtypeStruct((2, 512, 128), F32),
            jax.ShapeDtypeStruct((2, 128, 512), F32),
        ),
        in_specs=[vmem] * 5 + [anywhere] * 4,
        out_specs=(vmem,) * 3,
        scratch_shapes=[pltpu.VMEM(shape, kind) for shape, kind in buffers]
        + [dma((4,))]
        + [dma((5,))] * 4
        + [dma((N_SX,))] * 6
        + ring * 2,
        compiler_params=pltpu.CompilerParams(
            collective_id=0, has_side_effects=True, vmem_limit_bytes=VMEM_MIB * 1024 * 1024
        ),
        name="block",
    )(
        tokens[0],
        cotangent.reshape(512, 512),
        expert_ids.reshape(512, 1),
        scale,
        w_router,
        w_qkv,
        w_proj,
        w_up,
        w_down,
    )
    return (mixed.reshape(1, 16, 32, 512), grad_up, grad_down)


def solution(mesh):
    return jax.shard_map(
        on_device,
        mesh=mesh,
        in_specs=(
            P("dp", "sy", "sx", None),
            P("dp", "sy", "sx", None),
            P(),
            P(),
            P(),
            P(),
            P("sx", None, None),
            P("sx", None, None),
            P("dp", "sy", "sx", None, None),
        ),
        out_specs=(
            P("dp", "sy", "sx", None),
            P("sx", None, ("sy", "dp")),
            P("sx", ("sy", "dp"), None),
        ),
        check_vma=False,
    )
```

```python
import jax
import jax.numpy as jnp
from jax import lax
from jax.experimental import pallas as pl
from jax.experimental.pallas import tpu as pltpu
from jax.sharding import PartitionSpec as P

MESH = pl.DeviceIdType.MESH
BF16 = jnp.bfloat16
F32 = jnp.float32
N_SX = 16
VMEM_MIB = 52
CAP = 32
NEAR_FIRST = (0, 1, 15, 2, 14, 3, 13, 4, 12, 5, 11, 6, 10, 7, 9, 8)


def dot(a, b):
    return jnp.dot(a, b, preferred_element_type=F32)


def dot_tn(a, b):
    return lax.dot_general(a, b, (((0,), (0,)), ((), ())), preferred_element_type=F32)


def dot_nt(a, b):
    return lax.dot_general(a, b, (((1,), (1,)), ((), ())), preferred_element_type=F32)


def ring_places():
    sy, dp = lax.axis_index("sy"), lax.axis_index("dp")
    y, x = sy // 2, dp * 2 + lax.rem(sy, 2)
    to_x, to_y = [], []
    for step in (1, 3):
        nx, ny = lax.rem(x + step, 4), lax.rem(y + step, 4)
        to_x.append({"sy": y * 2 + lax.rem(nx, 2), "dp": nx // 2})
        to_y.append({"sy": ny * 2 + lax.rem(x, 2)})
    return x, y, to_x, to_y


def shard_of(x, y):
    return y * 4 + lax.rem(x, 2) * 2 + x // 2


class RingHalf:
    def __init__(self, full, part, cut, here_a, here_b, to_a, to_b, refs, out_at):
        self.full, self.part, self.cut = full, part, cut
        self.pa, self.pb = here_a, here_b
        self.to_a, self.to_b = to_a, to_b
        self.stage, self.bufs1, self.bufs2, self.hold = refs[:4]
        self.s1, self.r1, self.s2, self.r2 = refs[4:]
        self.out_at = out_at

    def order(self, k):
        return lax.rem(self.pb + 2 + k + (k // 2) * (1 + 2 * (k % 2)), 4)

    def copy1(self, kind, way, k):
        ref = self.bufs1.at[0, way, k] if kind == 2 else self.stage.at[kind, way, k]
        return pltpu.make_async_remote_copy(
            src_ref=ref,
            dst_ref=self.bufs1.at[kind, way, k],
            send_sem=self.s1.at[kind, way, k],
            recv_sem=self.r1.at[kind, way, k],
            device_id=self.to_a[way],
            device_id_type=MESH,
        )

    def copy2(self, kind, way):
        if kind == 0:
            ref = self.hold.at[0, way]
        elif kind == 1:
            ref = self.hold.at[1, 0] if way == 1 else self.hold.at[2, 1]
        else:
            ref = self.bufs2.at[0, way]
        return pltpu.make_async_remote_copy(
            src_ref=ref,
            dst_ref=self.bufs2.at[kind, way],
            send_sem=self.s2.at[kind, way],
            recv_sem=self.r2.at[kind, way],
            device_id=self.to_b[way],
            device_id_type=MESH,
        )

    def ahead(self, way):
        return lax.rem(self.pa + (1 if way == 0 else 3), 4)

    def send_own(self, k):
        far = self.full(lax.rem(self.pa + 2, 4), self.order(k)).astype(BF16)
        for way in range(2):
            self.stage[0, way, k] = self.cut(far, way)
            self.copy1(0, way, k).start()
        for way in range(2):
            part = self.part(1 - way, self.ahead(way), self.order(k))
            self.stage[1, way, k] = part.astype(BF16)
            self.copy1(1, way, k).start()

    def pass_on(self, k):
        for way in range(2):
            mine = self.part(way, self.ahead(way), self.order(k))
            self.copy1(0, way, k).wait_recv()
            self.bufs1[0, way, k] = (self.bufs1[0, way, k].astype(F32) + mine).astype(BF16)
            self.copy1(2, way, k).start()

    def close1(self, k):
        own = self.full(self.pa, self.order(k))
        for h in range(2):
            self.copy1(1, 1 - h, k).wait_recv()
            self.copy1(2, h, k).wait_recv()
            total = self.cut(own, h) + self.bufs1[1, 1 - h, k].astype(F32)
            total = total + self.bufs1[2, h, k].astype(F32)
            if k < 3:
                self.hold[k, h] = total.astype(BF16)
            else:
                self.out_at(h)[...] = total
        if k == 0:
            self.copy2(0, 0).start()
            self.copy2(0, 1).start()
        elif k == 1:
            self.copy2(1, 1).start()
        elif k == 2:
            self.copy2(1, 0).start()

    def pass_on2(self):
        for way in range(2):
            self.copy2(0, way).wait_recv()
            mine = self.hold[2 - way, way].astype(F32)
            self.bufs2[0, way] = (self.bufs2[0, way].astype(F32) + mine).astype(BF16)
            self.copy2(2, way).start()

    def close2(self):
        for h in range(2):
            self.copy2(1, 1 - h).wait_recv()
            self.copy2(2, h).wait_recv()
            out = self.out_at(h)
            out[...] = out[...] + self.bufs2[1, 1 - h].astype(F32) + self.bufs2[2, h].astype(F32)

    def finish(self):
        for kind in range(3):
            for way in range(2):
                for k in range(4):
                    self.copy1(kind, way, k).wait_send()
                self.copy2(kind, way).wait_send()


class Exchange:
    def __init__(self, me, away, source, landing, send_sem, recv_sem):
        self.me, self.away = me, away
        self.source, self.landing = source, landing
        self.send_sem, self.recv_sem = send_sem, recv_sem

    def peer(self, slot):
        d = NEAR_FIRST[slot]
        return lax.rem(self.me + (d if self.away else N_SX - d), N_SX)

    def copy(self, slot, e):
        peer = self.peer(slot)
        return pltpu.make_async_remote_copy(
            src_ref=self.source(slot, peer, e),
            dst_ref=self.landing(slot, self.me, e),
            send_sem=self.send_sem.at[e, slot],
            recv_sem=self.recv_sem.at[e, slot],
            device_id={"sx": peer},
            device_id_type=MESH,
        )


def gelu_parts(v):
    c = 0.7978845608028654
    sq = v * v
    t = jnp.tanh(c * v * (1.0 + 0.044715 * sq))
    half = 0.5 + 0.5 * t
    slope = half + (0.5 * c) * v * (1.0 - t * t) * (1.0 + (3 * 0.044715) * sq)
    return v * half, slope


def layer_norm(v):
    centred = v - jnp.mean(v, axis=-1, keepdims=True)
    return centred * lax.rsqrt(jnp.mean(centred * centred, axis=-1, keepdims=True) + 1e-05)


def split(v):
    high = v.astype(BF16)
    return high, (v - high.astype(F32)).astype(BF16)


def head_inverse(v, ones):
    high, low = split(v * v)
    total = dot(jnp.concatenate([high, low], axis=1), ones)
    return jnp.minimum(lax.rsqrt(total), 0.25)


def attend_group(qkv, joined, g, scale_ref, ones, same):
    part = [pl.ds(pl.multiple_of(n * 512 + g * 128, 128), 128) for n in range(3)]
    query, key, value = [qkv[:, p] for p in part]
    query = query * head_inverse(query, ones)
    k_high, k_low = split(key * head_inverse(key, ones))
    keys = jnp.concatenate([k_high, k_high, k_low], axis=1)
    value = value.astype(BF16)
    values = jnp.concatenate([value, jnp.ones_like(value)], axis=1)
    head = lax.shift_right_logical(lax.broadcasted_iota(jnp.int32, query.shape, 1), 5)
    top, bottom = jnp.zeros_like(query), jnp.ones_like(query)
    for i in range(4):
        q_high, q_low = split(jnp.where(head == i, query * scale_ref[4 * g + i], 0.0))
        scores = dot_nt(jnp.concatenate([q_high, q_low, q_high], axis=1), keys)
        weights = (jnp.exp(scores) * same).astype(BF16)
        out = dot(weights, values)
        top = jnp.where(head == i, out[:, :128], top)
        bottom = jnp.where(head == i, out[:, 128:], bottom)
    joined[:, part[0]] = (top / bottom).astype(BF16)


def block_kernel(
    tok_ref, cot_ref, ids_ref, scale_ref, router_ref, wqkv_any, wproj_any, wup_any, wdown_any,
    mixed_ref, oup_ref, odown_ref,
    wqkv, wproj, wup, wdown,
    resid, nsend, region, qkv, joined, attb, homeb, place, normed2,
    send, csend, recv, cotr, rgrad, rows_t, hidden, gact, back,
    us, u1, u2, uh, ds, d1, d2, dh,
    wsem, near, hs, hr, ks, kr, xs, xr, cs, cr, bs, br, *sems,
):
    me, sy = lax.axis_index("sx"), lax.axis_index("sy")
    n_sy = lax.axis_size("sy")
    x, y, to_x, to_y = ring_places()
    rows_out = Exchange(me, True, lambda s, p, e: send.at[e, p], lambda s, m, e: recv.at[e, s], xs, xr)
    cots_out = Exchange(me, True, lambda s, p, e: csend.at[e, p], lambda s, m, e: cotr.at[e, s], cs, cr)
    home = Exchange(me, False, lambda s, p, e: csend.at[e, s], lambda s, m, e: back.at[e, m], bs, br)
    below, above = lax.rem(sy + 1, n_sy), lax.rem(sy + n_sy - 1, n_sy)
    after, before = lax.rem(me + 1, N_SX), lax.rem(me + N_SX - 1, N_SX)
    onward = [{"sy": below}] * 3 + [{"sx": after}, {"sy": below, "sx": after}]
    backward = [{"sy": above}] * 3 + [{"sx": before}, {"sy": above, "sx": before}]
    greeted = to_x + to_y + [onward[0], onward[3], onward[4]]
    greeted += [backward[0], backward[3], backward[4]]
    barrier = pltpu.get_barrier_semaphore()
    for target in greeted:
        pl.semaphore_signal(barrier, inc=1, device_id=target, device_id_type=MESH)

    loads = [
        pltpu.make_async_copy(wqkv_any, wqkv, wsem.at[0]),
        pltpu.make_async_copy(wproj_any, wproj, wsem.at[1]),
        pltpu.make_async_copy(wup_any, wup, wsem.at[2]),
        pltpu.make_async_copy(wdown_any, wdown, wsem.at[3]),
    ]
    for load in loads:
        load.start()

    places = ((1, 0), (2, 0), (3, 0), (0, 1), (0, 0))

    def tile_at(cg, rh):
        return (slice(8 * rh, 8 * rh + 8), slice(8 * cg, 8 * cg + 8))

    resid[...] = tok_ref[...].astype(F32)
    for piece, (cg, rh) in enumerate(places):
        from_cg, from_rh = (cg + 3) % 4, 1 - rh
        block = layer_norm(resid[tile_at(from_cg, from_rh)].reshape(64, 512))
        nsend[piece] = block.astype(BF16)
    for cg in range(1, 4):
        block = layer_norm(resid[tile_at(cg - 1, 0)].reshape(64, 512))
        region[cg, 1] = block.astype(BF16)

    def halo(piece, forward):
        cg, rh = places[piece]
        return pltpu.make_async_remote_copy(
            src_ref=nsend.at[piece] if forward else attb.at[cg, rh],
            dst_ref=region.at[cg, rh] if forward else homeb.at[piece],
            send_sem=(hs if forward else ks).at[piece],
            recv_sem=(hr if forward else kr).at[piece],
            device_id=(onward if forward else backward)[piece],
            device_id_type=MESH,
        )

    pl.semaphore_wait(barrier, len(greeted))
    for piece in (1, 2, 0, 4, 3):
        halo(piece, True).start()

    def tell(r):
        for step in (2**r, N_SX - 2**r):
            peer = {"sx": lax.rem(me + step, N_SX)}
            pl.semaphore_signal(near.at[r], inc=1, device_id=peer, device_id_type=MESH)

    tell(0)

    ids = ids_ref[...]
    named = lax.broadcasted_iota(jnp.int32, (32, 512), 0) == ids
    earlier = lax.broadcasted_iota(jnp.int32, (512, 512), 0) < lax.broadcasted_iota(
        jnp.int32, (512, 512), 1
    )
    counts = dot(jnp.where(named, 1.0, 0.0).astype(BF16), jnp.where(earlier, 1.0, 0.0).astype(BF16))
    rank = jnp.sum(jnp.where(named, counts, 0.0), axis=0, keepdims=True)
    slot = jnp.bitwise_and(ids, 1) * 512 + lax.shift_right_logical(ids, 1) * CAP
    slot = slot.astype(F32) + rank
    for c in range(4):
        here = (lax.broadcasted_iota(jnp.int32, (256, 512), 0) + 256 * c).astype(F32)
        place[256 * c : 256 * c + 256] = jnp.where(here == slot, 1.0, 0.0).astype(BF16)
    pl.semaphore_wait(near.at[0], 2)
    tell(1)

    def gather(e, rows_ref, out_ref):
        rows = dot(place[512 * e : 512 * e + 512], rows_ref[...]).astype(BF16)
        out_ref[e] = rows.reshape(N_SX, CAP, 512)

    gather(0, cot_ref, csend)
    pl.semaphore_wait(near.at[1], 2)
    tell(2)
    gather(1, cot_ref, csend)
    pl.semaphore_wait(near.at[2], 2)
    for e in range(2):
        for s in range(1, N_SX):
            cots_out.copy(s, e).start()
        cotr[e, 0] = csend[e, me]

    lane = lax.shift_right_logical(lax.broadcasted_iota(jnp.int32, (256, 128), 1), 5)
    row = lax.shift_right_logical(
        jnp.bitwise_and(lax.broadcasted_iota(jnp.int32, (256, 128), 0), 127), 5
    )
    ones = jnp.where(lane == row, 1.0, 0.0).astype(BF16)

    loads[0].wait()
    loads[1].wait()
    row_cut = jnp.where(sy == 0, 1, 0)
    for w in (1, 0):
        for piece in (1, 2) if w else (0, 4, 3):
            halo(piece, True).wait_recv()
        qkv[...] = dot(region[2 * w : 2 * w + 2].reshape(256, 512), wqkv[...])
        col_cut = jnp.where(me == 0, 1 - w, 0)

        def label(axis):
            b = lax.shift_right_logical(lax.broadcasted_iota(jnp.int32, (256, 256), axis), 6)
            return jnp.bitwise_and(b, 1) * (2 * row_cut) + lax.shift_right_logical(b, 1) * col_cut

        same = jnp.where(label(0) == label(1), 1.0, 0.0)

        def group(g, carry):
            attend_group(qkv, joined, g, scale_ref, ones, same)
            return carry

        lax.fori_loop(0, 4, group, 0)
        attended = dot(joined[...], wproj[...]).astype(BF16)
        attb[2 * w : 2 * w + 2] = attended.reshape(2, 2, 64, 512)
        for piece in (1, 2) if w else (0, 4, 3):
            halo(piece, False).start()
        for cg in (2, 3) if w else (1,):
            resid[tile_at(cg - 1, 0)] += attb[cg, 1].astype(F32).reshape(8, 8, 512)
    for piece in (1, 2, 0, 4, 3):
        cg, rh = places[piece]
        halo(piece, False).wait_recv()
        at = tile_at((cg + 3) % 4, 1 - rh)
        resid[at] += homeb[piece].astype(F32).reshape(8, 8, 512)
    for c in range(4):
        rows = layer_norm(resid[4 * c : 4 * c + 4].reshape(128, 512))
        normed2[128 * c : 128 * c + 128] = rows.astype(BF16)
    for e in range(2):
        gather(e, normed2, send)
        for s in range(1, N_SX):
            rows_out.copy(s, e).start()
        recv[e, 0] = send[e, me]
    loads[2].wait()
    loads[3].wait()
    for e in range(2):
        for s in range(1, N_SX):
            cots_out.copy(s, e).wait_send()

    def hidden_part(e):
        for s in range(1, N_SX):
            cots_out.copy(s, e).wait_recv()
            rows_out.copy(s, e).wait_recv()
        rows = recv[e].reshape(512, 512)
        logits = dot_nt(rows, router_ref[...])
        column = lax.broadcasted_iota(jnp.int32, logits.shape, 1) == 2 * me + e
        gate = jax.nn.sigmoid(jnp.sum(jnp.where(column, logits, 0.0), axis=1, keepdims=True))
        rgrad[e] = (gate * cotr[e].reshape(512, 512).astype(F32)).astype(BF16)
        rows_t[e] = rows.T

        def step(f, carry):
            part = pl.ds(pl.multiple_of(f * 256, 256), 256)
            act = dot(recv[e].reshape(512, 512), wup[e, :, part])
            hid, slope = gelu_parts(act)
            hidden[e, :, part] = hid.astype(BF16)
            through = dot_nt(rgrad[e], wdown[e, part, :])
            gact[e, :, part] = (through * slope).astype(BF16)
            return carry

        lax.fori_loop(0, 8, step, 0)

    def return_part(e):
        out = dot(hidden[e], wdown[e]).astype(BF16)
        csend[e] = out.reshape(N_SX, CAP, 512)
        for s in range(1, N_SX):
            home.copy(s, e).start()
        back[e, me] = csend[e, 0]

    def halves_of(e):
        def columns(ix, iy):
            return pl.ds(pl.multiple_of(shard_of(ix, iy) * 128, 128), 128)

        def up_full(ix, iy):
            return dot(rows_t[e], gact[e, :, columns(ix, iy)])

        def up_part(h, ix, iy):
            return dot(rows_t[e, 256 * h : 256 * h + 256], gact[e, :, columns(ix, iy)])

        def down_full(iy, ix):
            return dot_tn(hidden[e, :, columns(ix, iy)], rgrad[e])

        def down_part(h, iy, ix):
            return dot_tn(hidden[e, :, columns(ix, iy)], rgrad[e, :, 256 * h : 256 * h + 256])

        up_refs = [ref.at[e] for ref in (us, u1, u2, uh) + sems[:4]]
        down_refs = [ref.at[e] for ref in (ds, d1, d2, dh) + sems[4:]]
        return (
            RingHalf(
                up_full, up_part, lambda v, h: v[256 * h : 256 * h + 256],
                x, y, to_x, to_y, up_refs, lambda h: oup_ref.at[e, pl.ds(256 * h, 256)],
            ),
            RingHalf(
                down_full, down_part, lambda v, h: v[:, 256 * h : 256 * h + 256],
                y, x, to_y, to_x, down_refs, lambda h: odown_ref.at[e, :, pl.ds(256 * h, 256)],
            ),
        )

    first, second = halves_of(0), halves_of(1)

    def each(halves, method):
        def step(k, carry):
            for half in halves:
                getattr(half, method)(k)
            return carry

        lax.fori_loop(0, 4, step, 0)

    def close(halves):
        for k in range(4):
            for half in halves:
                half.close1(k)

    hidden_part(0)
    each(first, "send_own")
    each(first, "pass_on")
    hidden_part(1)
    each(second, "send_own")
    close(first)
    return_part(0)
    return_part(1)
    each(second, "pass_on")
    for half in first:
        half.pass_on2()
    close(second)
    for half in second:
        half.pass_on2()
    logits = dot_nt(router_ref[...], normed2[...])
    gate = jax.nn.sigmoid(jnp.sum(jnp.where(named, logits, 0.0), axis=0, keepdims=True))
    same_token = lax.broadcasted_iota(jnp.int32, (512, 512), 0) == lax.broadcasted_iota(
        jnp.int32, (512, 512), 1
    )
    gate = jnp.sum(jnp.where(same_token, gate, 0.0), axis=1, keepdims=True)
    for e in range(2):
        for s in range(1, N_SX):
            home.copy(s, e).wait_recv()
    moe = dot_tn(place[...], back[...].reshape(1024, 512))
    mixed_ref[...] = (resid[...].reshape(512, 512) + gate * moe).astype(BF16)
    for half in first + second:
        half.close2()
    for half in first + second:
        half.finish()
    for e in range(2):
        for s in range(1, N_SX):
            rows_out.copy(s, e).wait_send()
            home.copy(s, e).wait_send()
    for piece in range(5):
        halo(piece, True).wait_send()
        halo(piece, False).wait_send()


def on_device(tokens, cotangent, w_qkv, w_proj, logit_scale, w_router, w_up, w_down, expert_ids):
    dma = pltpu.SemaphoreType.DMA
    vmem = pl.BlockSpec(memory_space=pltpu.VMEM)
    anywhere = pl.BlockSpec(memory_space=pl.ANY)
    ring = [dma((2, 3, 2, 4)), dma((2, 3, 2, 4)), dma((2, 3, 2)), dma((2, 3, 2))]
    buffers = [
        ((512, 1536), BF16),
        ((512, 512), BF16),
        ((2, 512, 2048), BF16),
        ((2, 2048, 512), BF16),
        ((16, 32, 512), F32),
        ((5, 64, 512), BF16),
        ((4, 2, 64, 512), BF16),
        ((256, 1536), F32),
        ((256, 512), BF16),
        ((4, 2, 64, 512), BF16),
        ((5, 64, 512), BF16),
        ((1024, 512), BF16),
        ((512, 512), BF16),
        ((2, N_SX, CAP, 512), BF16),
        ((2, N_SX, CAP, 512), BF16),
        ((2, N_SX, CAP, 512), BF16),
        ((2, N_SX, CAP, 512), BF16),
        ((2, 512, 512), BF16),
        ((2, 512, 512), BF16),
        ((2, 512, 2048), BF16),
        ((2, 512, 2048), BF16),
        ((2, N_SX, CAP, 512), BF16),
        ((2, 2, 2, 4, 256, 128), BF16),
        ((2, 3, 2, 4, 256, 128), BF16),
        ((2, 3, 2, 256, 128), BF16),
        ((2, 3, 2, 256, 128), BF16),
        ((2, 2, 2, 4, 128, 256), BF16),
        ((2, 3, 2, 4, 128, 256), BF16),
        ((2, 3, 2, 128, 256), BF16),
        ((2, 3, 2, 128, 256), BF16),
    ]
    mixed, grad_up, grad_down = pl.pallas_call(
        block_kernel,
        out_shape=(
            jax.ShapeDtypeStruct((512, 512), BF16),
            jax.ShapeDtypeStruct((2, 512, 128), F32),
            jax.ShapeDtypeStruct((2, 128, 512), F32),
        ),
        in_specs=[vmem] * 3 + [pl.BlockSpec(memory_space=pltpu.SMEM), vmem] + [anywhere] * 4,
        out_specs=(vmem,) * 3,
        scratch_shapes=[pltpu.VMEM(shape, kind) for shape, kind in buffers]
        + [dma((4,)), pltpu.SemaphoreType.REGULAR((3,))]
        + [dma((5,))] * 4
        + [dma((2, N_SX))] * 6
        + ring * 2,
        compiler_params=pltpu.CompilerParams(
            collective_id=0, has_side_effects=True, vmem_limit_bytes=VMEM_MIB * 1024 * 1024
        ),
        name="block",
    )(
        tokens[0],
        cotangent.reshape(512, 512),
        expert_ids.reshape(1, 512),
        logit_scale,
        w_router.T,
        w_qkv,
        w_proj,
        w_up,
        w_down,
    )
    return (mixed.reshape(1, 16, 32, 512), grad_up, grad_down)


def solution(mesh):
    return jax.shard_map(
        on_device,
        mesh=mesh,
        in_specs=(
            P("dp", "sy", "sx", None),
            P("dp", "sy", "sx", None),
            P(),
            P(),
            P(),
            P(),
            P("sx", None, None),
            P("sx", None, None),
            P("dp", "sy", "sx", None, None),
        ),
        out_specs=(
            P("dp", "sy", "sx", None),
            P("sx", None, ("sy", "dp")),
            P("sx", ("sy", "dp"), None),
        ),
        check_vma=False,
    )
```

```python
import jax
import jax.numpy as jnp
from jax import lax
from jax.experimental import pallas as pl
from jax.experimental.pallas import tpu as pltpu
from jax.sharding import PartitionSpec as P

MESH = pl.DeviceIdType.MESH
BF16 = jnp.bfloat16
F32 = jnp.float32
N_SX = 16
VMEM_MIB = 52
CAP = 32
NEAR_FIRST = (0, 1, 15, 2, 14, 3, 13, 4, 12, 5, 11, 6, 10, 7, 9, 8)


def dot(a, b):
    return jnp.dot(a, b, preferred_element_type=F32)


def dot_tn(a, b):
    return lax.dot_general(a, b, (((0,), (0,)), ((), ())), preferred_element_type=F32)


def dot_nt(a, b):
    return lax.dot_general(a, b, (((1,), (1,)), ((), ())), preferred_element_type=F32)


def ring_places():
    sy, dp = lax.axis_index("sy"), lax.axis_index("dp")
    y, x = sy // 2, dp * 2 + lax.rem(sy, 2)
    to_x, to_y = [], []
    for step in (1, 3):
        nx, ny = lax.rem(x + step, 4), lax.rem(y + step, 4)
        to_x.append({"sy": y * 2 + lax.rem(nx, 2), "dp": nx // 2})
        to_y.append({"sy": ny * 2 + lax.rem(x, 2)})
    return x, y, to_x, to_y


def shard_of(x, y):
    return y * 4 + lax.rem(x, 2) * 2 + x // 2


class RingHalf:
    def __init__(self, fill, here_a, here_b, to_a, to_b, refs, out_at):
        self.fill = fill
        self.pa, self.pb = here_a, here_b
        self.to_a, self.to_b = to_a, to_b
        self.mine, self.bufs1, self.bufs2, self.hold = refs[:4]
        self.s1, self.r1, self.s2, self.r2 = refs[4:]
        self.out_at = out_at

    def rank_of(self, ib):
        d = lax.rem(ib - self.pb + 4, 4)
        return (d // 2) * (d - 2) + (1 - d // 2) * (3 - d)

    def chunk(self, d):
        self.fill(self.mine.at[d], lax.rem(self.pa + d, 4), self.rank_of)

    def copy1(self, kind, way, kk):
        two = pl.ds(2 * kk, 2)
        if kind == 0:
            ref = self.mine.at[2, way, two]
        elif kind == 1:
            ref = self.mine.at[1 + 2 * way, 1 - way, two]
        else:
            ref = self.bufs1.at[0, way, two]
        return pltpu.make_async_remote_copy(
            src_ref=ref,
            dst_ref=self.bufs1.at[kind, way, two],
            send_sem=self.s1,
            recv_sem=self.r1.at[kind, way, kk],
            device_id=self.to_a[way],
            device_id_type=MESH,
        )

    def copy2(self, kind, way):
        if kind == 0:
            ref = self.hold.at[0, way]
        elif kind == 1:
            ref = self.hold.at[1, 0] if way == 1 else self.hold.at[2, 1]
        else:
            ref = self.bufs2.at[0, way]
        return pltpu.make_async_remote_copy(
            src_ref=ref,
            dst_ref=self.bufs2.at[kind, way],
            send_sem=self.s2,
            recv_sem=self.r2.at[kind, way],
            device_id=self.to_b[way],
            device_id_type=MESH,
        )

    def send_far(self):
        self.chunk(2)
        for kk in range(2):
            for way in range(2):
                self.copy1(0, way, kk).start()

    def send_raw(self):
        for way in range(2):
            self.chunk(1 + 2 * way)
            for kk in range(2):
                self.copy1(1, way, kk).start()

    def keep_own(self):
        self.chunk(0)

    def pass_on(self, kk):
        for way in range(2):
            self.copy1(0, way, kk).wait_recv()
            for k in (2 * kk, 2 * kk + 1):
                own = self.mine[1 + 2 * way, way, k].astype(F32)
                self.bufs1[0, way, k] = (self.bufs1[0, way, k].astype(F32) + own).astype(BF16)
            self.copy1(2, way, kk).start()

    def close1(self, kk):
        for h in range(2):
            self.copy1(1, 1 - h, kk).wait_recv()
            self.copy1(2, h, kk).wait_recv()
        for k in (2 * kk, 2 * kk + 1):
            for h in range(2):
                total = self.mine[0, h, k].astype(F32) + self.bufs1[1, 1 - h, k].astype(F32)
                total = total + self.bufs1[2, h, k].astype(F32)
                if k < 3:
                    self.hold[k, h] = total.astype(BF16)
                else:
                    self.out_at(h)[...] = total
            if k == 0:
                self.copy2(0, 0).start()
                self.copy2(0, 1).start()
            elif k == 1:
                self.copy2(1, 1).start()
            elif k == 2:
                self.copy2(1, 0).start()

    def pass_on2(self):
        for way in range(2):
            self.copy2(0, way).wait_recv()
            own = self.hold[2 - way, way].astype(F32)
            self.bufs2[0, way] = (self.bufs2[0, way].astype(F32) + own).astype(BF16)
            self.copy2(2, way).start()

    def close2(self):
        for h in range(2):
            self.copy2(1, 1 - h).wait_recv()
            self.copy2(2, h).wait_recv()
            out = self.out_at(h)
            out[...] = out[...] + self.bufs2[1, 1 - h].astype(F32) + self.bufs2[2, h].astype(F32)

    def finish(self):
        pltpu.make_async_copy(self.bufs1, self.bufs1, self.s1).wait()
        pltpu.make_async_copy(self.bufs2, self.bufs2, self.s2).wait()


class Exchange:
    def __init__(self, me, away, source, landing, send_sem, recv_sem):
        self.me, self.away = me, away
        self.source, self.landing = source, landing
        self.send_sem, self.recv_sem = send_sem, recv_sem

    def peer(self, slot):
        d = NEAR_FIRST[slot]
        return lax.rem(self.me + (d if self.away else N_SX - d), N_SX)

    def start(self):
        for slot in range(1, N_SX):
            peer = self.peer(slot)
            pltpu.make_async_remote_copy(
                src_ref=self.source(slot, peer),
                dst_ref=self.landing(slot, self.me),
                send_sem=self.send_sem,
                recv_sem=self.recv_sem,
                device_id={"sx": peer},
                device_id_type=MESH,
            ).start()

    def wait(self, whole, sem):
        pltpu.make_async_copy(whole, whole, sem).wait()


def gelu_parts(v):
    c = 0.7978845608028654
    sq = v * v
    t = jnp.tanh(c * v * (1.0 + 0.044715 * sq))
    half = 0.5 + 0.5 * t
    slope = half + (0.5 * c) * v * (1.0 - t * t) * (1.0 + (3 * 0.044715) * sq)
    return v * half, slope


def layer_norm(v):
    centred = v - jnp.mean(v, axis=-1, keepdims=True)
    return centred * lax.rsqrt(jnp.mean(centred * centred, axis=-1, keepdims=True) + 1e-05)


def split(v):
    high = v.astype(BF16)
    return high, (v - high.astype(F32)).astype(BF16)


def head_inverse(v, ones):
    high, low = split(v * v)
    total = dot(jnp.concatenate([high, low], axis=1), ones)
    return jnp.minimum(lax.rsqrt(total), 0.25)


def attend_group(qkv, joined, g, scale_ref, ones, same):
    part = [pl.ds(pl.multiple_of(n * 512 + g * 128, 128), 128) for n in range(3)]
    query, key, value = [qkv[:, p] for p in part]
    query = query * head_inverse(query, ones)
    k_high, k_low = split(key * head_inverse(key, ones))
    keys = jnp.concatenate([k_high, k_high, k_low], axis=1)
    value = value.astype(BF16)
    values = jnp.concatenate([value, jnp.ones_like(value)], axis=1)
    head = lax.shift_right_logical(lax.broadcasted_iota(jnp.int32, query.shape, 1), 5)
    top, bottom = jnp.zeros_like(query), jnp.ones_like(query)
    for i in range(4):
        q_high, q_low = split(jnp.where(head == i, query * scale_ref[4 * g + i], 0.0))
        scores = dot_nt(jnp.concatenate([q_high, q_low, q_high], axis=1), keys)
        weights = (jnp.exp(scores) * same).astype(BF16)
        out = dot(weights, values)
        top = jnp.where(head == i, out[:, :128], top)
        bottom = jnp.where(head == i, out[:, 128:], bottom)
    joined[:, part[0]] = (top / bottom).astype(BF16)


def block_kernel(
    tok_ref, cot_ref, ids_ref, scale_ref, router_ref, wqkv_any, wproj_any, wup_any, wdown_any,
    mixed_ref, oup_ref, odown_ref,
    wqkv, wproj, wup, wdown,
    resid, nsend, region, qkv, joined, attb, homeb, place, normed2,
    send, csend, recv, cotr, rgrad, rows_t, hidden, gact, back,
    us, u1, u2, uh, ds, d1, d2, dh,
    wsem, hs, hr, ks, kr, xs, xr, cs, cr, bs, br, *sems,
):
    me, sy = lax.axis_index("sx"), lax.axis_index("sy")
    n_sy = lax.axis_size("sy")
    x, y, to_x, to_y = ring_places()
    rows_out = [
        Exchange(
            me, True,
            lambda s, p, e=e: send.at[e, p], lambda s, m, e=e: recv.at[e, s], xs.at[e], xr.at[e],
        )
        for e in range(2)
    ]
    cots_out = Exchange(
        me, True, lambda s, p: csend.at[:, p], lambda s, m: cotr.at[:, s], cs.at[0], cr.at[0]
    )
    home = Exchange(
        me, False, lambda s, p: csend.at[:, s], lambda s, m: back.at[:, m], bs.at[0], br.at[0]
    )
    others = pl.ds(1, N_SX - 1)
    below, above = lax.rem(sy + 1, n_sy), lax.rem(sy + n_sy - 1, n_sy)
    after, before = lax.rem(me + 1, N_SX), lax.rem(me + N_SX - 1, N_SX)
    onward = [{"sy": below}] * 3 + [{"sx": after}, {"sy": below, "sx": after}]
    backward = [{"sy": above}] * 3 + [{"sx": before}, {"sy": above, "sx": before}]
    greeted = [{"sx": rows_out[0].peer(s)} for s in range(1, N_SX)] + to_x + to_y
    greeted += [onward[0], onward[4], backward[0], backward[4]]
    barrier = pltpu.get_barrier_semaphore()
    for target in greeted:
        pl.semaphore_signal(barrier, inc=1, device_id=target, device_id_type=MESH)

    loads = [
        pltpu.make_async_copy(wqkv_any, wqkv, wsem.at[0]),
        pltpu.make_async_copy(wproj_any, wproj, wsem.at[1]),
        pltpu.make_async_copy(wup_any, wup, wsem.at[2]),
        pltpu.make_async_copy(wdown_any, wdown, wsem.at[3]),
    ]
    for load in loads:
        load.start()

    places = ((1, 0), (2, 0), (3, 0), (0, 1), (0, 0))

    def tile_at(cg, rh):
        return (slice(8 * rh, 8 * rh + 8), slice(8 * cg, 8 * cg + 8))

    resid[...] = tok_ref[...].astype(F32)
    for piece, (cg, rh) in enumerate(places):
        from_cg, from_rh = (cg + 3) % 4, 1 - rh
        block = layer_norm(resid[tile_at(from_cg, from_rh)].reshape(64, 512))
        nsend[piece] = block.astype(BF16)
    for cg in range(1, 4):
        block = layer_norm(resid[tile_at(cg - 1, 0)].reshape(64, 512))
        region[cg, 1] = block.astype(BF16)

    def halo(piece, forward):
        cg, rh = places[piece]
        return pltpu.make_async_remote_copy(
            src_ref=nsend.at[piece] if forward else attb.at[cg, rh],
            dst_ref=region.at[cg, rh] if forward else homeb.at[piece],
            send_sem=(hs if forward else ks).at[piece],
            recv_sem=(hr if forward else kr).at[piece],
            device_id=(onward if forward else backward)[piece],
            device_id_type=MESH,
        )

    pl.semaphore_wait(barrier, len(greeted))
    for piece in (1, 2, 0, 4, 3):
        halo(piece, True).start()

    ids = ids_ref[...]
    named = lax.broadcasted_iota(jnp.int32, (32, 512), 0) == ids
    earlier = lax.broadcasted_iota(jnp.int32, (512, 512), 0) < lax.broadcasted_iota(
        jnp.int32, (512, 512), 1
    )
    counts = dot(jnp.where(named, 1.0, 0.0).astype(BF16), jnp.where(earlier, 1.0, 0.0).astype(BF16))
    rank = jnp.sum(jnp.where(named, counts, 0.0), axis=0, keepdims=True)
    slot = jnp.bitwise_and(ids, 1) * 512 + lax.shift_right_logical(ids, 1) * CAP
    slot = slot.astype(F32) + rank
    for c in range(4):
        here = (lax.broadcasted_iota(jnp.int32, (256, 512), 0) + 256 * c).astype(F32)
        place[256 * c : 256 * c + 256] = jnp.where(here == slot, 1.0, 0.0).astype(BF16)

    def gather(e, rows_ref, out_ref):
        rows = dot(place[512 * e : 512 * e + 512], rows_ref[...]).astype(BF16)
        out_ref[e] = rows.reshape(N_SX, CAP, 512)

    gather(0, cot_ref, csend)
    gather(1, cot_ref, csend)
    cots_out.start()
    for e in range(2):
        cotr[e, 0] = csend[e, me]

    lane = lax.shift_right_logical(lax.broadcasted_iota(jnp.int32, (256, 128), 1), 5)
    row = lax.shift_right_logical(
        jnp.bitwise_and(lax.broadcasted_iota(jnp.int32, (256, 128), 0), 127), 5
    )
    ones = jnp.where(lane == row, 1.0, 0.0).astype(BF16)

    loads[0].wait()
    loads[1].wait()
    row_cut = jnp.where(sy == 0, 1, 0)
    for w in (1, 0):
        for piece in (1, 2) if w else (0, 4, 3):
            halo(piece, True).wait_recv()
        qkv[...] = dot(region[2 * w : 2 * w + 2].reshape(256, 512), wqkv[...])
        col_cut = jnp.where(me == 0, 1 - w, 0)

        def label(axis):
            b = lax.shift_right_logical(lax.broadcasted_iota(jnp.int32, (256, 256), axis), 6)
            return jnp.bitwise_and(b, 1) * (2 * row_cut) + lax.shift_right_logical(b, 1) * col_cut

        same = jnp.where(label(0) == label(1), 1.0, 0.0)

        def group(g, carry):
            attend_group(qkv, joined, g, scale_ref, ones, same)
            return carry

        lax.fori_loop(0, 4, group, 0)
        attended = dot(joined[...], wproj[...]).astype(BF16)
        attb[2 * w : 2 * w + 2] = attended.reshape(2, 2, 64, 512)
        for piece in (1, 2) if w else (0, 4, 3):
            halo(piece, False).start()
        for cg in (2, 3) if w else (1,):
            resid[tile_at(cg - 1, 0)] += attb[cg, 1].astype(F32).reshape(8, 8, 512)
    for piece in (1, 2, 0, 4, 3):
        cg, rh = places[piece]
        halo(piece, False).wait_recv()
        at = tile_at((cg + 3) % 4, 1 - rh)
        resid[at] += homeb[piece].astype(F32).reshape(8, 8, 512)
    for c in range(4):
        rows = layer_norm(resid[4 * c : 4 * c + 4].reshape(128, 512))
        normed2[128 * c : 128 * c + 128] = rows.astype(BF16)
    for e in range(2):
        gather(e, normed2, send)
        rows_out[e].start()
        recv[e, 0] = send[e, me]
    loads[2].wait()
    loads[3].wait()
    cots_out.wait(csend.at[:, others], cs.at[0])
    cots_out.wait(cotr.at[:, others], cr.at[0])

    def hidden_part(e):
        rows_out[e].wait(recv.at[e, others], xr.at[e])
        rows = recv[e].reshape(512, 512)
        logits = dot_nt(rows, router_ref[...])
        column = lax.broadcasted_iota(jnp.int32, logits.shape, 1) == 2 * me + e
        gate = jax.nn.sigmoid(jnp.sum(jnp.where(column, logits, 0.0), axis=1, keepdims=True))
        rgrad[e] = (gate * cotr[e].reshape(512, 512).astype(F32)).astype(BF16)
        rows_t[e] = rows.T

        def step(f, carry):
            part = pl.ds(pl.multiple_of(f * 256, 256), 256)
            act = dot(recv[e].reshape(512, 512), wup[e, :, part])
            hid, slope = gelu_parts(act)
            hidden[e, :, part] = hid.astype(BF16)
            through = dot_nt(rgrad[e], wdown[e, part, :])
            grad = (through * slope).astype(BF16)
            for n in range(2):
                col = (lax.rem(f, 2) * 2 + n) * 512 + (f // 2) * 128
                col = pl.multiple_of(col, 128)
                gact[e, :, pl.ds(col, 128)] = grad[:, 128 * n : 128 * n + 128]
            return carry

        lax.fori_loop(0, 8, step, 0)

    def return_part(e):
        out = dot(hidden[e], wdown[e]).astype(BF16)
        csend[e] = out.reshape(N_SX, CAP, 512)
        back[e, me] = csend[e, 0]

    def x_of(q):
        return (q % 2) * 2 + q // 2

    def halves_of(e):
        def fill_up(to, ix, rank_of):
            q = lax.rem(ix, 2) * 2 + ix // 2
            all_y = dot(rows_t[e], gact[e, :, pl.ds(pl.multiple_of(q * 512, 512), 512)])
            for iy in range(4):
                for h in range(2):
                    part = all_y[256 * h : 256 * h + 256, 128 * iy : 128 * iy + 128]
                    to[h, rank_of(iy)] = part.astype(BF16)

        def fill_down(to, iy, rank_of):
            hid = hidden[e, :, pl.ds(pl.multiple_of(iy * 512, 512), 512)]
            all_x = dot_tn(hid, rgrad[e])
            for q in range(4):
                for h in range(2):
                    part = all_x[128 * q : 128 * q + 128, 256 * h : 256 * h + 256]
                    to[h, rank_of(x_of(q))] = part.astype(BF16)

        up_refs = [ref.at[e] for ref in (us, u1, u2, uh) + sems[:4]]
        down_refs = [ref.at[e] for ref in (ds, d1, d2, dh) + sems[4:]]
        return (
            RingHalf(
                fill_up, x, y, to_x, to_y, up_refs, lambda h: oup_ref.at[e, pl.ds(256 * h, 256)]
            ),
            RingHalf(
                fill_down, y, x, to_y, to_x, down_refs,
                lambda h: odown_ref.at[e, :, pl.ds(256 * h, 256)],
            ),
        )

    first, second = halves_of(0), halves_of(1)

    def each(halves, method, *steps):
        for step in steps or ((),):
            for half in halves:
                getattr(half, method)(*step)

    hidden_part(0)
    each(first, "send_far")
    each(first, "send_raw")
    each(first, "pass_on", (0,), (1,))
    each(first, "keep_own")
    hidden_part(1)
    each(second, "send_far")
    each(second, "send_raw")
    each(first, "close1", (0,), (1,))
    return_part(0)
    return_part(1)
    home.start()
    each(second, "pass_on", (0,), (1,))
    each(first, "pass_on2")
    each(second, "keep_own")
    each(second, "close1", (0,), (1,))
    each(second, "pass_on2")
    logits = dot_nt(router_ref[...], normed2[...])
    gate = jax.nn.sigmoid(jnp.sum(jnp.where(named, logits, 0.0), axis=0, keepdims=True))
    same_token = lax.broadcasted_iota(jnp.int32, (512, 512), 0) == lax.broadcasted_iota(
        jnp.int32, (512, 512), 1
    )
    gate = jnp.sum(jnp.where(same_token, gate, 0.0), axis=1, keepdims=True)
    home.wait(back.at[:, others], br.at[0])
    moe = dot_tn(place[...], back[...].reshape(1024, 512))
    mixed_ref[...] = (resid[...].reshape(512, 512) + gate * moe).astype(BF16)
    for half in first + second:
        half.close2()
    for half in first + second:
        half.finish()
    for e in range(2):
        rows_out[e].wait(send.at[e, others], xs.at[e])
    home.wait(csend.at[:, others], bs.at[0])
    for piece in range(5):
        halo(piece, True).wait_send()
        halo(piece, False).wait_send()


def on_device(tokens, cotangent, w_qkv, w_proj, logit_scale, w_router, w_up, w_down, expert_ids):
    dma = pltpu.SemaphoreType.DMA
    vmem = pl.BlockSpec(memory_space=pltpu.VMEM)
    anywhere = pl.BlockSpec(memory_space=pl.ANY)
    ring = [dma((2,)), dma((2, 3, 2, 2)), dma((2,)), dma((2, 3, 2))]
    buffers = [
        ((512, 1536), BF16),
        ((512, 512), BF16),
        ((2, 512, 2048), BF16),
        ((2, 2048, 512), BF16),
        ((16, 32, 512), F32),
        ((5, 64, 512), BF16),
        ((4, 2, 64, 512), BF16),
        ((256, 1536), F32),
        ((256, 512), BF16),
        ((4, 2, 64, 512), BF16),
        ((5, 64, 512), BF16),
        ((1024, 512), BF16),
        ((512, 512), BF16),
        ((2, N_SX, CAP, 512), BF16),
        ((2, N_SX, CAP, 512), BF16),
        ((2, N_SX, CAP, 512), BF16),
        ((2, N_SX, CAP, 512), BF16),
        ((2, 512, 512), BF16),
        ((2, 512, 512), BF16),
        ((2, 512, 2048), BF16),
        ((2, 512, 2048), BF16),
        ((2, N_SX, CAP, 512), BF16),
        ((2, 4, 2, 4, 256, 128), BF16),
        ((2, 3, 2, 4, 256, 128), BF16),
        ((2, 3, 2, 256, 128), BF16),
        ((2, 3, 2, 256, 128), BF16),
        ((2, 4, 2, 4, 128, 256), BF16),
        ((2, 3, 2, 4, 128, 256), BF16),
        ((2, 3, 2, 128, 256), BF16),
        ((2, 3, 2, 128, 256), BF16),
    ]
    mixed, grad_up, grad_down = pl.pallas_call(
        block_kernel,
        out_shape=(
            jax.ShapeDtypeStruct((512, 512), BF16),
            jax.ShapeDtypeStruct((2, 512, 128), F32),
            jax.ShapeDtypeStruct((2, 128, 512), F32),
        ),
        in_specs=[vmem] * 3 + [pl.BlockSpec(memory_space=pltpu.SMEM), vmem] + [anywhere] * 4,
        out_specs=(vmem,) * 3,
        scratch_shapes=[pltpu.VMEM(shape, kind) for shape, kind in buffers]
        + [dma((4,))]
        + [dma((5,))] * 4
        + [dma((2,))] * 6
        + ring * 2,
        compiler_params=pltpu.CompilerParams(
            collective_id=0, has_side_effects=True, vmem_limit_bytes=VMEM_MIB * 1024 * 1024
        ),
        name="block",
    )(
        tokens[0],
        cotangent.reshape(512, 512),
        expert_ids.reshape(1, 512),
        logit_scale,
        w_router.T,
        w_qkv,
        w_proj,
        w_up,
        w_down,
    )
    return (mixed.reshape(1, 16, 32, 512), grad_up, grad_down)


def solution(mesh):
    return jax.shard_map(
        on_device,
        mesh=mesh,
        in_specs=(
            P("dp", "sy", "sx", None),
            P("dp", "sy", "sx", None),
            P(),
            P(),
            P(),
            P(),
            P("sx", None, None),
            P("sx", None, None),
            P("dp", "sy", "sx", None, None),
        ),
        out_specs=(
            P("dp", "sy", "sx", None),
            P("sx", None, ("sy", "dp")),
            P("sx", ("sy", "dp"), None),
        ),
        check_vma=False,
    )
```

```python
import jax
import jax.numpy as jnp
from jax import lax
from jax.experimental import pallas as pl
from jax.experimental.pallas import tpu as pltpu
from jax.sharding import PartitionSpec as P

MESH = pl.DeviceIdType.MESH
BF16 = jnp.bfloat16
F32 = jnp.float32
N_SX = 16
VMEM_MIB = 52
CAP = 32
NEAR_FIRST = (0, 1, 15, 2, 14, 3, 13, 4, 12, 5, 11, 6, 10, 7, 9, 8)


def dot(a, b):
    return jnp.dot(a, b, preferred_element_type=F32)


def dot_tn(a, b):
    return lax.dot_general(a, b, (((0,), (0,)), ((), ())), preferred_element_type=F32)


def dot_nt(a, b):
    return lax.dot_general(a, b, (((1,), (1,)), ((), ())), preferred_element_type=F32)


def ring_places():
    sy, dp = lax.axis_index("sy"), lax.axis_index("dp")
    y, x = sy // 2, dp * 2 + lax.rem(sy, 2)
    to_x, to_y = [], []
    for step in (1, 3):
        nx, ny = lax.rem(x + step, 4), lax.rem(y + step, 4)
        to_x.append({"sy": y * 2 + lax.rem(nx, 2), "dp": nx // 2})
        to_y.append({"sy": ny * 2 + lax.rem(x, 2)})
    return x, y, to_x, to_y


def shard_of(x, y):
    return y * 4 + lax.rem(x, 2) * 2 + x // 2


class RingHalf:
    def __init__(self, fill, here_a, here_b, to_a, to_b, refs, out_at):
        self.fill = fill
        self.pa, self.pb = here_a, here_b
        self.to_a, self.to_b = to_a, to_b
        self.mine, self.bufs1, self.bufs2, self.hold = refs[:4]
        self.s1, self.r1, self.s2, self.r2 = refs[4:]
        self.out_at = out_at

    def rank_of(self, ib):
        d = lax.rem(ib - self.pb + 4, 4)
        return (d // 2) * (d - 2) + (1 - d // 2) * (3 - d)

    def chunk(self, d):
        self.fill(self.mine.at[d], lax.rem(self.pa + d, 4), self.rank_of)

    def copy1(self, kind, way, kk):
        two = pl.ds(2 * kk, 2)
        if kind == 0:
            ref = self.mine.at[2, way, two]
        elif kind == 1:
            ref = self.mine.at[1 + 2 * way, 1 - way, two]
        else:
            ref = self.bufs1.at[0, way, two]
        return pltpu.make_async_remote_copy(
            src_ref=ref,
            dst_ref=self.bufs1.at[kind, way, two],
            send_sem=self.s1,
            recv_sem=self.r1.at[kind, way, kk],
            device_id=self.to_a[way],
            device_id_type=MESH,
        )

    def copy2(self, kind, way):
        if kind == 0:
            ref = self.hold.at[0, way]
        elif kind == 1:
            ref = self.hold.at[1, 0] if way == 1 else self.hold.at[2, 1]
        else:
            ref = self.bufs2.at[0, way]
        return pltpu.make_async_remote_copy(
            src_ref=ref,
            dst_ref=self.bufs2.at[kind, way],
            send_sem=self.s2,
            recv_sem=self.r2.at[kind, way],
            device_id=self.to_b[way],
            device_id_type=MESH,
        )

    def send_far(self):
        self.chunk(2)
        for kk in range(2):
            for way in range(2):
                self.copy1(0, way, kk).start()

    def send_raw(self):
        for way in range(2):
            self.chunk(1 + 2 * way)
            for kk in range(2):
                self.copy1(1, way, kk).start()

    def keep_own(self):
        self.chunk(0)

    def pass_on(self, kk):
        for way in range(2):
            self.copy1(0, way, kk).wait_recv()
            for k in (2 * kk, 2 * kk + 1):
                own = self.mine[1 + 2 * way, way, k].astype(F32)
                self.bufs1[0, way, k] = (self.bufs1[0, way, k].astype(F32) + own).astype(BF16)
            self.copy1(2, way, kk).start()

    def close1(self, kk):
        for h in range(2):
            self.copy1(1, 1 - h, kk).wait_recv()
            self.copy1(2, h, kk).wait_recv()
        for k in (2 * kk, 2 * kk + 1):
            for h in range(2):
                total = self.mine[0, h, k].astype(F32) + self.bufs1[1, 1 - h, k].astype(F32)
                total = total + self.bufs1[2, h, k].astype(F32)
                if k < 3:
                    self.hold[k, h] = total.astype(BF16)
                else:
                    self.out_at(h)[...] = total
            if k == 0:
                self.copy2(0, 0).start()
                self.copy2(0, 1).start()
            elif k == 1:
                self.copy2(1, 1).start()
            elif k == 2:
                self.copy2(1, 0).start()

    def pass_on2(self):
        for way in range(2):
            self.copy2(0, way).wait_recv()
            own = self.hold[2 - way, way].astype(F32)
            self.bufs2[0, way] = (self.bufs2[0, way].astype(F32) + own).astype(BF16)
            self.copy2(2, way).start()

    def close2(self):
        for h in range(2):
            self.copy2(1, 1 - h).wait_recv()
            self.copy2(2, h).wait_recv()
            out = self.out_at(h)
            out[...] = out[...] + self.bufs2[1, 1 - h].astype(F32) + self.bufs2[2, h].astype(F32)

    def finish(self):
        pltpu.make_async_copy(self.bufs1, self.bufs1, self.s1).wait()
        pltpu.make_async_copy(self.bufs2, self.bufs2, self.s2).wait()


class Exchange:
    def __init__(self, me, away, source, landing, send_sem, recv_sem):
        self.me, self.away = me, away
        self.source, self.landing = source, landing
        self.send_sem, self.recv_sem = send_sem, recv_sem

    def peer(self, slot):
        d = NEAR_FIRST[slot]
        return lax.rem(self.me + (d if self.away else N_SX - d), N_SX)

    def start(self):
        for slot in range(1, N_SX):
            peer = self.peer(slot)
            pltpu.make_async_remote_copy(
                src_ref=self.source(slot, peer),
                dst_ref=self.landing(slot, self.me),
                send_sem=self.send_sem,
                recv_sem=self.recv_sem,
                device_id={"sx": peer},
                device_id_type=MESH,
            ).start()

    def wait(self, whole, sem):
        pltpu.make_async_copy(whole, whole, sem).wait()


def gelu_parts(v):
    c = 0.7978845608028654
    sq = v * v
    t = jnp.tanh(c * v * (1.0 + 0.044715 * sq))
    half = 0.5 + 0.5 * t
    slope = half + (0.5 * c) * v * (1.0 - t * t) * (1.0 + (3 * 0.044715) * sq)
    return v * half, slope


def layer_norm(v):
    centred = v - jnp.mean(v, axis=-1, keepdims=True)
    return centred * lax.rsqrt(jnp.mean(centred * centred, axis=-1, keepdims=True) + 1e-05)


def split(v):
    high = v.astype(BF16)
    return high, (v - high.astype(F32)).astype(BF16)


def head_inverse(v, ones):
    high, low = split(v * v)
    total = dot(jnp.concatenate([high, low], axis=1), ones)
    return jnp.minimum(lax.rsqrt(total), 0.25)


def attend_group(qkv, joined, g, scale_ref, ones, same):
    part = [pl.ds(pl.multiple_of(n * 512 + g * 128, 128), 128) for n in range(3)]
    query, key, value = [qkv[:, p] for p in part]
    query = query * head_inverse(query, ones)
    k_high, k_low = split(key * head_inverse(key, ones))
    keys = jnp.concatenate([k_high, k_high, k_low], axis=1)
    value = value.astype(BF16)
    values = jnp.concatenate([value, jnp.ones_like(value)], axis=1)
    head = lax.shift_right_logical(lax.broadcasted_iota(jnp.int32, query.shape, 1), 5)
    top, bottom = jnp.zeros_like(query), jnp.ones_like(query)
    for i in range(4):
        q_high, q_low = split(jnp.where(head == i, query * scale_ref[4 * g + i], 0.0))
        scores = dot_nt(jnp.concatenate([q_high, q_low, q_high], axis=1), keys)
        weights = (jnp.exp(scores) * same).astype(BF16)
        out = dot(weights, values)
        top = jnp.where(head == i, out[:, :128], top)
        bottom = jnp.where(head == i, out[:, 128:], bottom)
    joined[:, part[0]] = (top / bottom).astype(BF16)


def block_kernel(
    tok_any, cot_any, ids_any, scale_any, router_any, wqkv_any, wproj_any, wup_any, wdown_any,
    mixed_ref, oup_ref, odown_ref,
    tok_ref, cot_ref, ids_ref, scale_ref, router_ref, wqkv, wproj, wup, wdown,
    resid, nsend, region, qkv, joined, attb, homeb, place, normed2,
    send, csend, recv, cotr, rgrad, rows_t, hidden, gact, back,
    us, u1, u2, uh, ds, d1, d2, dh,
    wsem, hs, hr, ks, kr, xs, xr, cs, cr, bs, br, *sems,
):
    me, sy = lax.axis_index("sx"), lax.axis_index("sy")
    n_sy = lax.axis_size("sy")
    x, y, to_x, to_y = ring_places()
    rows_out = [
        Exchange(
            me, True,
            lambda s, p, e=e: send.at[e, p], lambda s, m, e=e: recv.at[e, s], xs.at[e], xr.at[e],
        )
        for e in range(2)
    ]
    cots_out = Exchange(
        me, True, lambda s, p: csend.at[:, p], lambda s, m: cotr.at[:, s], cs.at[0], cr.at[0]
    )
    home = Exchange(
        me, False, lambda s, p: csend.at[:, s], lambda s, m: back.at[:, m], bs.at[0], br.at[0]
    )
    others = pl.ds(1, N_SX - 1)
    below, above = lax.rem(sy + 1, n_sy), lax.rem(sy + n_sy - 1, n_sy)
    after, before = lax.rem(me + 1, N_SX), lax.rem(me + N_SX - 1, N_SX)
    onward = [{"sy": below}] * 3 + [{"sx": after}, {"sy": below, "sx": after}]
    backward = [{"sy": above}] * 3 + [{"sx": before}, {"sy": above, "sx": before}]
    greeted = [{"sx": rows_out[0].peer(s)} for s in range(1, N_SX)] + to_x + to_y
    greeted += [onward[0], onward[4], backward[0], backward[4]]
    barrier = pltpu.get_barrier_semaphore()
    for target in greeted:
        pl.semaphore_signal(barrier, inc=1, device_id=target, device_id_type=MESH)

    pairs = (
        (wqkv_any, wqkv),
        (wproj_any, wproj),
        (wup_any, wup),
        (wdown_any, wdown),
        (tok_any, tok_ref),
        (ids_any, ids_ref),
        (cot_any, cot_ref),
        (scale_any, scale_ref),
        (router_any, router_ref),
    )
    loads = [pltpu.make_async_copy(a, b, wsem.at[n]) for n, (a, b) in enumerate(pairs)]
    for n in (4, 5, 6, 7, 8, 0, 1, 2, 3):
        loads[n].start()

    places = ((1, 0), (2, 0), (3, 0), (0, 1), (0, 0))

    def tile_at(cg, rh):
        return (slice(8 * rh, 8 * rh + 8), slice(8 * cg, 8 * cg + 8))

    loads[4].wait()
    resid[...] = tok_ref[...].astype(F32)
    for piece, (cg, rh) in enumerate(places):
        from_cg, from_rh = (cg + 3) % 4, 1 - rh
        block = layer_norm(resid[tile_at(from_cg, from_rh)].reshape(64, 512))
        nsend[piece] = block.astype(BF16)
    for cg in range(1, 4):
        block = layer_norm(resid[tile_at(cg - 1, 0)].reshape(64, 512))
        region[cg, 1] = block.astype(BF16)

    def halo(piece, forward):
        cg, rh = places[piece]
        return pltpu.make_async_remote_copy(
            src_ref=nsend.at[piece] if forward else attb.at[cg, rh],
            dst_ref=region.at[cg, rh] if forward else homeb.at[piece],
            send_sem=(hs if forward else ks).at[piece],
            recv_sem=(hr if forward else kr).at[piece],
            device_id=(onward if forward else backward)[piece],
            device_id_type=MESH,
        )

    pl.semaphore_wait(barrier, len(greeted))
    for piece in (1, 2, 0, 4, 3):
        halo(piece, True).start()

    loads[5].wait()
    ids = ids_ref[...]
    named = lax.broadcasted_iota(jnp.int32, (32, 512), 0) == ids
    earlier = lax.broadcasted_iota(jnp.int32, (512, 512), 0) < lax.broadcasted_iota(
        jnp.int32, (512, 512), 1
    )
    counts = dot(jnp.where(named, 1.0, 0.0).astype(BF16), jnp.where(earlier, 1.0, 0.0).astype(BF16))
    rank = jnp.sum(jnp.where(named, counts, 0.0), axis=0, keepdims=True)
    slot = jnp.bitwise_and(ids, 1) * 512 + lax.shift_right_logical(ids, 1) * CAP
    slot = slot.astype(F32) + rank
    for c in range(4):
        here = (lax.broadcasted_iota(jnp.int32, (256, 512), 0) + 256 * c).astype(F32)
        place[256 * c : 256 * c + 256] = jnp.where(here == slot, 1.0, 0.0).astype(BF16)

    def gather(e, rows_ref, out_ref):
        rows = dot(place[512 * e : 512 * e + 512], rows_ref[...]).astype(BF16)
        out_ref[e] = rows.reshape(N_SX, CAP, 512)

    loads[6].wait()
    gather(0, cot_ref, csend)
    gather(1, cot_ref, csend)
    cots_out.start()
    for e in range(2):
        cotr[e, 0] = csend[e, me]

    lane = lax.shift_right_logical(lax.broadcasted_iota(jnp.int32, (256, 128), 1), 5)
    row = lax.shift_right_logical(
        jnp.bitwise_and(lax.broadcasted_iota(jnp.int32, (256, 128), 0), 127), 5
    )
    ones = jnp.where(lane == row, 1.0, 0.0).astype(BF16)

    for n in (0, 1, 7, 8):
        loads[n].wait()
    row_cut = jnp.where(sy == 0, 1, 0)
    for w in (1, 0):
        for piece in (1, 2) if w else (0, 4, 3):
            halo(piece, True).wait_recv()
        qkv[...] = dot(region[2 * w : 2 * w + 2].reshape(256, 512), wqkv[...])
        col_cut = jnp.where(me == 0, 1 - w, 0)

        def label(axis):
            b = lax.shift_right_logical(lax.broadcasted_iota(jnp.int32, (256, 256), axis), 6)
            return jnp.bitwise_and(b, 1) * (2 * row_cut) + lax.shift_right_logical(b, 1) * col_cut

        same = jnp.where(label(0) == label(1), 1.0, 0.0)

        def group(g, carry):
            attend_group(qkv, joined, g, scale_ref, ones, same)
            return carry

        lax.fori_loop(0, 4, group, 0)
        attended = dot(joined[...], wproj[...]).astype(BF16)
        attb[2 * w : 2 * w + 2] = attended.reshape(2, 2, 64, 512)
        for piece in (1, 2) if w else (0, 4, 3):
            halo(piece, False).start()
        for cg in (2, 3) if w else (1,):
            resid[tile_at(cg - 1, 0)] += attb[cg, 1].astype(F32).reshape(8, 8, 512)
    for piece in (1, 2, 0, 4, 3):
        cg, rh = places[piece]
        halo(piece, False).wait_recv()
        at = tile_at((cg + 3) % 4, 1 - rh)
        resid[at] += homeb[piece].astype(F32).reshape(8, 8, 512)
    for c in range(4):
        rows = layer_norm(resid[4 * c : 4 * c + 4].reshape(128, 512))
        normed2[128 * c : 128 * c + 128] = rows.astype(BF16)
    for e in range(2):
        gather(e, normed2, send)
        if e:
            rows_out[0].wait(send.at[0, others], xs.at[0])
        rows_out[e].start()
        recv[e, 0] = send[e, me]
    loads[2].wait()
    loads[3].wait()
    cots_out.wait(csend.at[:, others], cs.at[0])
    cots_out.wait(cotr.at[:, others], cr.at[0])

    def hidden_part(e):
        rows_out[e].wait(recv.at[e, others], xr.at[e])
        rows = recv[e].reshape(512, 512)
        logits = dot_nt(rows, router_ref[...])
        column = lax.broadcasted_iota(jnp.int32, logits.shape, 1) == 2 * me + e
        gate = jax.nn.sigmoid(jnp.sum(jnp.where(column, logits, 0.0), axis=1, keepdims=True))
        rgrad[e] = (gate * cotr[e].reshape(512, 512).astype(F32)).astype(BF16)
        rows_t[e] = rows.T

        def step(f, carry):
            part = pl.ds(pl.multiple_of(f * 256, 256), 256)
            act = dot(recv[e].reshape(512, 512), wup[e, :, part])
            hid, slope = gelu_parts(act)
            hidden[e, :, part] = hid.astype(BF16)
            through = dot_nt(rgrad[e], wdown[e, part, :])
            grad = (through * slope).astype(BF16)
            for n in range(2):
                col = (lax.rem(f, 2) * 2 + n) * 512 + (f // 2) * 128
                col = pl.multiple_of(col, 128)
                gact[e, :, pl.ds(col, 128)] = grad[:, 128 * n : 128 * n + 128]
            return carry

        lax.fori_loop(0, 8, step, 0)

    def return_part(e):
        out = dot(hidden[e], wdown[e]).astype(BF16)
        csend[e] = out.reshape(N_SX, CAP, 512)
        back[e, me] = csend[e, 0]

    def x_of(q):
        return (q % 2) * 2 + q // 2

    def halves_of(e):
        def fill_up(to, ix, rank_of):
            q = lax.rem(ix, 2) * 2 + ix // 2
            all_y = dot(rows_t[e], gact[e, :, pl.ds(pl.multiple_of(q * 512, 512), 512)])
            for iy in range(4):
                for h in range(2):
                    part = all_y[256 * h : 256 * h + 256, 128 * iy : 128 * iy + 128]
                    to[h, rank_of(iy)] = part.astype(BF16)

        def fill_down(to, iy, rank_of):
            hid = hidden[e, :, pl.ds(pl.multiple_of(iy * 512, 512), 512)]
            all_x = dot_tn(hid, rgrad[e])
            for q in range(4):
                for h in range(2):
                    part = all_x[128 * q : 128 * q + 128, 256 * h : 256 * h + 256]
                    to[h, rank_of(x_of(q))] = part.astype(BF16)

        up_refs = [ref.at[e] for ref in (us, u1, u2, uh) + sems[:4]]
        down_refs = [ref.at[e] for ref in (ds, d1, d2, dh) + sems[4:]]
        return (
            RingHalf(
                fill_up, x, y, to_x, to_y, up_refs, lambda h: oup_ref.at[e, pl.ds(256 * h, 256)]
            ),
            RingHalf(
                fill_down, y, x, to_y, to_x, down_refs,
                lambda h: odown_ref.at[e, :, pl.ds(256 * h, 256)],
            ),
        )

    first, second = halves_of(0), halves_of(1)

    def each(halves, method, *steps):
        for step in steps or ((),):
            for half in halves:
                getattr(half, method)(*step)

    hidden_part(0)
    each(first, "send_far")
    each(first, "send_raw")
    each(first, "pass_on", (0,), (1,))
    each(first, "keep_own")
    hidden_part(1)
    each(second, "send_far")
    each(second, "send_raw")
    each(first, "close1", (0,), (1,))
    return_part(0)
    return_part(1)
    home.start()
    each(second, "pass_on", (0,), (1,))
    each(first, "pass_on2")
    each(second, "keep_own")
    each(second, "close1", (0,), (1,))
    each(second, "pass_on2")
    logits = dot_nt(router_ref[...], normed2[...])
    gate = jax.nn.sigmoid(jnp.sum(jnp.where(named, logits, 0.0), axis=0, keepdims=True))
    same_token = lax.broadcasted_iota(jnp.int32, (512, 512), 0) == lax.broadcasted_iota(
        jnp.int32, (512, 512), 1
    )
    gate = jnp.sum(jnp.where(same_token, gate, 0.0), axis=1, keepdims=True)
    home.wait(back.at[:, others], br.at[0])
    moe = dot_tn(place[...], back[...].reshape(1024, 512))
    mixed_ref[...] = (resid[...].reshape(512, 512) + gate * moe).astype(BF16)
    for half in first + second:
        half.close2()
    for half in first + second:
        half.finish()
    rows_out[1].wait(send.at[1, others], xs.at[1])
    home.wait(csend.at[:, others], bs.at[0])
    for piece in range(5):
        halo(piece, True).wait_send()
        halo(piece, False).wait_send()


def on_device(tokens, cotangent, w_qkv, w_proj, logit_scale, w_router, w_up, w_down, expert_ids):
    dma = pltpu.SemaphoreType.DMA
    vmem = pl.BlockSpec(memory_space=pltpu.VMEM)
    hbm = pl.BlockSpec(memory_space=pltpu.HBM)
    ring = [dma((2,)), dma((2, 3, 2, 2)), dma((2,)), dma((2, 3, 2))]
    buffers = [
        ((16, 32, 512), BF16),
        ((512, 512), BF16),
        ((1, 512), jnp.int32),
        None,
        ((32, 512), BF16),
        ((512, 1536), BF16),
        ((512, 512), BF16),
        ((2, 512, 2048), BF16),
        ((2, 2048, 512), BF16),
        ((16, 32, 512), F32),
        ((5, 64, 512), BF16),
        ((4, 2, 64, 512), BF16),
        ((256, 1536), F32),
        ((256, 512), BF16),
        ((4, 2, 64, 512), BF16),
        ((5, 64, 512), BF16),
        ((1024, 512), BF16),
        ((512, 512), BF16),
        ((2, N_SX, CAP, 512), BF16),
        ((2, N_SX, CAP, 512), BF16),
        ((2, N_SX, CAP, 512), BF16),
        ((2, N_SX, CAP, 512), BF16),
        ((2, 512, 512), BF16),
        ((2, 512, 512), BF16),
        ((2, 512, 2048), BF16),
        ((2, 512, 2048), BF16),
        ((2, N_SX, CAP, 512), BF16),
        ((2, 4, 2, 4, 256, 128), BF16),
        ((2, 3, 2, 4, 256, 128), BF16),
        ((2, 3, 2, 256, 128), BF16),
        ((2, 3, 2, 256, 128), BF16),
        ((2, 4, 2, 4, 128, 256), BF16),
        ((2, 3, 2, 4, 128, 256), BF16),
        ((2, 3, 2, 128, 256), BF16),
        ((2, 3, 2, 128, 256), BF16),
    ]
    mixed, grad_up, grad_down = pl.pallas_call(
        block_kernel,
        out_shape=(
            jax.ShapeDtypeStruct((512, 512), BF16),
            jax.ShapeDtypeStruct((2, 512, 128), F32),
            jax.ShapeDtypeStruct((2, 128, 512), F32),
        ),
        in_specs=[hbm] * 9,
        out_specs=(vmem,) * 3,
        scratch_shapes=[pltpu.VMEM(*b) if b else pltpu.SMEM((16,), F32) for b in buffers]
        + [dma((9,))]
        + [dma((5,))] * 4
        + [dma((2,))] * 6
        + ring * 2,
        compiler_params=pltpu.CompilerParams(
            collective_id=0, has_side_effects=True, vmem_limit_bytes=VMEM_MIB * 1024 * 1024
        ),
        name="block",
    )(
        tokens[0],
        cotangent.reshape(512, 512),
        expert_ids.reshape(1, 512),
        logit_scale,
        w_router.T,
        w_qkv,
        w_proj,
        w_up,
        w_down,
    )
    return (mixed.reshape(1, 16, 32, 512), grad_up, grad_down)


def solution(mesh):
    return jax.shard_map(
        on_device,
        mesh=mesh,
        in_specs=(
            P("dp", "sy", "sx", None),
            P("dp", "sy", "sx", None),
            P(),
            P(),
            P(),
            P(),
            P("sx", None, None),
            P("sx", None, None),
            P("dp", "sy", "sx", None, None),
        ),
        out_specs=(
            P("dp", "sy", "sx", None),
            P("sx", None, ("sy", "dp")),
            P("sx", ("sy", "dp"), None),
        ),
        check_vma=False,
    )
```

```python
import jax
import jax.numpy as jnp
from jax import lax
from jax.experimental import pallas as pl
from jax.experimental.pallas import tpu as pltpu
from jax.sharding import PartitionSpec as P

MESH = pl.DeviceIdType.MESH
BF16 = jnp.bfloat16
F32 = jnp.float32
N_SX = 16
VMEM_MIB = 52
CAP = 32
NEAR_FIRST = (0, 1, 15, 2, 14, 3, 13, 4, 12, 5, 11, 6, 10, 7, 9, 8)


def dot(a, b):
    return jnp.dot(a, b, preferred_element_type=F32)


def dot_tn(a, b):
    return lax.dot_general(a, b, (((0,), (0,)), ((), ())), preferred_element_type=F32)


def dot_nt(a, b):
    return lax.dot_general(a, b, (((1,), (1,)), ((), ())), preferred_element_type=F32)


def ring_places():
    sy, dp = lax.axis_index("sy"), lax.axis_index("dp")
    y, x = sy // 2, dp * 2 + lax.rem(sy, 2)
    to_x, to_y = [], []
    for step in (1, 3):
        nx, ny = lax.rem(x + step, 4), lax.rem(y + step, 4)
        to_x.append({"sy": y * 2 + lax.rem(nx, 2), "dp": nx // 2})
        to_y.append({"sy": ny * 2 + lax.rem(x, 2)})
    return x, y, to_x, to_y


def shard_of(x, y):
    return y * 4 + lax.rem(x, 2) * 2 + x // 2


class RingHalf:
    def __init__(self, fill, here_a, here_b, to_a, to_b, refs, out_at):
        self.fill = fill
        self.pa, self.pb = here_a, here_b
        self.to_a, self.to_b = to_a, to_b
        self.mine, self.bufs1, self.bufs2, self.hold = refs[:4]
        self.s1, self.r1, self.s2, self.r2 = refs[4:]
        self.out_at = out_at

    def rank_of(self, ib):
        d = lax.rem(ib - self.pb + 4, 4)
        return (d // 2) * (d - 2) + (1 - d // 2) * (3 - d)

    def chunk(self, d):
        self.fill(self.mine.at[d], lax.rem(self.pa + d, 4), self.rank_of)

    def copy1(self, kind, way, kk):
        two = pl.ds(2 * kk, 2)
        if kind == 0:
            ref = self.mine.at[2, way, two]
        elif kind == 1:
            ref = self.mine.at[1 + 2 * way, 1 - way, two]
        else:
            ref = self.bufs1.at[0, way, two]
        return pltpu.make_async_remote_copy(
            src_ref=ref,
            dst_ref=self.bufs1.at[kind, way, two],
            send_sem=self.s1,
            recv_sem=self.r1.at[kind, way, kk],
            device_id=self.to_a[way],
            device_id_type=MESH,
        )

    def copy2(self, kind, way):
        if kind == 0:
            ref = self.hold.at[0, way]
        elif kind == 1:
            ref = self.hold.at[1, 0] if way == 1 else self.hold.at[2, 1]
        else:
            ref = self.bufs2.at[0, way]
        return pltpu.make_async_remote_copy(
            src_ref=ref,
            dst_ref=self.bufs2.at[kind, way],
            send_sem=self.s2,
            recv_sem=self.r2.at[kind, way],
            device_id=self.to_b[way],
            device_id_type=MESH,
        )

    def send_far(self):
        self.chunk(2)
        for kk in range(2):
            for way in range(2):
                self.copy1(0, way, kk).start()

    def send_raw(self):
        for way in range(2):
            self.chunk(1 + 2 * way)
            for kk in range(2):
                self.copy1(1, way, kk).start()

    def keep_own(self):
        self.chunk(0)

    def pass_on(self, kk):
        for way in range(2):
            self.copy1(0, way, kk).wait_recv()
            for k in (2 * kk, 2 * kk + 1):
                own = self.mine[1 + 2 * way, way, k].astype(F32)
                self.bufs1[0, way, k] = (self.bufs1[0, way, k].astype(F32) + own).astype(BF16)
            self.copy1(2, way, kk).start()

    def close1(self, kk):
        for h in range(2):
            self.copy1(1, 1 - h, kk).wait_recv()
            self.copy1(2, h, kk).wait_recv()
        for k in (2 * kk, 2 * kk + 1):
            for h in range(2):
                total = self.mine[0, h, k].astype(F32) + self.bufs1[1, 1 - h, k].astype(F32)
                total = total + self.bufs1[2, h, k].astype(F32)
                if k < 3:
                    self.hold[k, h] = total.astype(BF16)
                else:
                    self.out_at(h)[...] = total
            if k == 0:
                self.copy2(0, 0).start()
                self.copy2(0, 1).start()
            elif k == 1:
                self.copy2(1, 1).start()
            elif k == 2:
                self.copy2(1, 0).start()

    def pass_on2(self):
        for way in range(2):
            self.copy2(0, way).wait_recv()
            own = self.hold[2 - way, way].astype(F32)
            self.bufs2[0, way] = (self.bufs2[0, way].astype(F32) + own).astype(BF16)
            self.copy2(2, way).start()

    def close2(self):
        for h in range(2):
            self.copy2(1, 1 - h).wait_recv()
            self.copy2(2, h).wait_recv()
            out = self.out_at(h)
            out[...] = out[...] + self.bufs2[1, 1 - h].astype(F32) + self.bufs2[2, h].astype(F32)

    def finish(self):
        pltpu.make_async_copy(self.bufs1, self.bufs1, self.s1).wait()
        pltpu.make_async_copy(self.bufs2, self.bufs2, self.s2).wait()


class Exchange:
    def __init__(self, me, away, source, landing, send_sem, recv_sem):
        self.me, self.away = me, away
        self.source, self.landing = source, landing
        self.send_sem, self.recv_sem = send_sem, recv_sem

    def peer(self, slot):
        d = NEAR_FIRST[slot]
        return lax.rem(self.me + (d if self.away else N_SX - d), N_SX)

    def start(self):
        for slot in range(1, N_SX):
            peer = self.peer(slot)
            pltpu.make_async_remote_copy(
                src_ref=self.source(slot, peer),
                dst_ref=self.landing(slot, self.me),
                send_sem=self.send_sem,
                recv_sem=self.recv_sem,
                device_id={"sx": peer},
                device_id_type=MESH,
            ).start()

    def wait(self, whole, sem):
        pltpu.make_async_copy(whole, whole, sem).wait()


def gelu_parts(v):
    c = 0.7978845608028654
    sq = v * v
    t = jnp.tanh(c * v * (1.0 + 0.044715 * sq))
    half = 0.5 + 0.5 * t
    slope = half + (0.5 * c) * v * (1.0 - t * t) * (1.0 + (3 * 0.044715) * sq)
    return v * half, slope


def layer_norm(v):
    centred = v - jnp.mean(v, axis=-1, keepdims=True)
    return centred * lax.rsqrt(jnp.mean(centred * centred, axis=-1, keepdims=True) + 1e-05)


def split(v):
    high = v.astype(BF16)
    return high, (v - high.astype(F32)).astype(BF16)


def head_inverse(v, ones):
    high, low = split(v * v)
    total = dot(jnp.concatenate([high, low], axis=1), ones)
    return jnp.minimum(lax.rsqrt(total), 0.25)


def attend_group(qkv, joined, g, scale_ref, ones, same):
    part = [pl.ds(pl.multiple_of(n * 512 + g * 128, 128), 128) for n in range(3)]
    query, key, value = [qkv[:, p] for p in part]
    query = query * head_inverse(query, ones)
    k_high, k_low = split(key * head_inverse(key, ones))
    keys = jnp.concatenate([k_high, k_high, k_low], axis=1)
    value = value.astype(BF16)
    values = jnp.concatenate([value, jnp.ones_like(value)], axis=1)
    head = lax.shift_right_logical(lax.broadcasted_iota(jnp.int32, query.shape, 1), 5)
    top, bottom = jnp.zeros_like(query), jnp.ones_like(query)
    for i in range(4):
        q_high, q_low = split(jnp.where(head == i, query * scale_ref[4 * g + i], 0.0))
        scores = dot_nt(jnp.concatenate([q_high, q_low, q_high], axis=1), keys)
        weights = (jnp.exp(scores) * same).astype(BF16)
        out = dot(weights, values)
        top = jnp.where(head == i, out[:, :128], top)
        bottom = jnp.where(head == i, out[:, 128:], bottom)
    joined[:, part[0]] = (top / bottom).astype(BF16)


def block_kernel(
    tok_any, cot_any, ids_any, scale_any, router_any, wqkv_any, wproj_any, wup_any, wdown_any,
    mixed_ref, oup_ref, odown_ref,
    tok_ref, cot_ref, ids_ref, scale_ref, router_ref, wqkv, wproj, wup, wdown,
    resid, nsend, region, qkv, joined, attb, homeb, place, normed2,
    send, csend, recv, cotr, rgrad, rows_t, hidden, gact, back,
    us, u1, u2, uh, ds, d1, d2, dh,
    wsem, hs, hr, ks, kr, xs, xr, cs, cr, bs, br, *sems,
):
    me, sy = lax.axis_index("sx"), lax.axis_index("sy")
    n_sy = lax.axis_size("sy")
    x, y, to_x, to_y = ring_places()
    rows_out = [
        Exchange(
            me, True,
            lambda s, p, e=e: send.at[e, p], lambda s, m, e=e: recv.at[e, s], xs.at[e], xr.at[e],
        )
        for e in range(2)
    ]
    cots_out = Exchange(
        me, True, lambda s, p: csend.at[:, p], lambda s, m: cotr.at[:, s], cs.at[0], cr.at[0]
    )
    home = Exchange(
        me, False, lambda s, p: csend.at[:, s], lambda s, m: back.at[:, m], bs.at[0], br.at[0]
    )
    others = pl.ds(1, N_SX - 1)
    below, above = lax.rem(sy + 1, n_sy), lax.rem(sy + n_sy - 1, n_sy)
    after, before = lax.rem(me + 1, N_SX), lax.rem(me + N_SX - 1, N_SX)
    onward = [{"sy": below}] * 3 + [{"sx": after}, {"sy": below, "sx": after}]
    backward = [{"sy": above}] * 3 + [{"sx": before}, {"sy": above, "sx": before}]
    greeted = [{"sx": rows_out[0].peer(s)} for s in range(1, N_SX)] + to_x + to_y
    greeted += [onward[0], onward[4], backward[0], backward[4]]
    barrier = pltpu.get_barrier_semaphore()
    for target in greeted:
        pl.semaphore_signal(barrier, inc=1, device_id=target, device_id_type=MESH)

    pairs = (
        (wqkv_any, wqkv),
        (wproj_any, wproj),
        (wup_any, wup),
        (wdown_any, wdown),
        (tok_any, tok_ref),
        (ids_any, ids_ref),
        (cot_any, cot_ref),
        (scale_any, scale_ref),
        (router_any, router_ref),
    )
    loads = [pltpu.make_async_copy(a, b, wsem.at[n]) for n, (a, b) in enumerate(pairs)]
    for n in (4, 5, 6, 7, 8, 0, 1, 2, 3):
        loads[n].start()

    places = ((1, 0), (2, 0), (3, 0), (0, 1), (0, 0))

    def tile_at(cg, rh):
        return (slice(8 * rh, 8 * rh + 8), slice(8 * cg, 8 * cg + 8))

    loads[4].wait()
    resid[...] = tok_ref[...].astype(F32)
    for piece, (cg, rh) in enumerate(places):
        from_cg, from_rh = (cg + 3) % 4, 1 - rh
        block = layer_norm(resid[tile_at(from_cg, from_rh)].reshape(64, 512))
        nsend[piece] = block.astype(BF16)
    for cg in range(1, 4):
        block = layer_norm(resid[tile_at(cg - 1, 0)].reshape(64, 512))
        region[cg, 1] = block.astype(BF16)

    def halo(piece, forward):
        cg, rh = places[piece]
        return pltpu.make_async_remote_copy(
            src_ref=nsend.at[piece] if forward else attb.at[cg, rh],
            dst_ref=region.at[cg, rh] if forward else homeb.at[piece],
            send_sem=(hs if forward else ks).at[piece],
            recv_sem=(hr if forward else kr).at[piece],
            device_id=(onward if forward else backward)[piece],
            device_id_type=MESH,
        )

    pl.semaphore_wait(barrier, len(greeted))
    for piece in (1, 2, 0, 4, 3):
        halo(piece, True).start()

    loads[5].wait()
    ids = ids_ref[...]
    named = lax.broadcasted_iota(jnp.int32, (32, 512), 0) == ids
    earlier = lax.broadcasted_iota(jnp.int32, (512, 512), 0) < lax.broadcasted_iota(
        jnp.int32, (512, 512), 1
    )
    counts = dot(jnp.where(named, 1.0, 0.0).astype(BF16), jnp.where(earlier, 1.0, 0.0).astype(BF16))
    rank = jnp.sum(jnp.where(named, counts, 0.0), axis=0, keepdims=True)
    slot = jnp.bitwise_and(ids, 1) * 512 + lax.shift_right_logical(ids, 1) * CAP
    slot = slot.astype(F32) + rank
    for c in range(4):
        here = (lax.broadcasted_iota(jnp.int32, (256, 512), 0) + 256 * c).astype(F32)
        place[256 * c : 256 * c + 256] = jnp.where(here == slot, 1.0, 0.0).astype(BF16)

    def gather(e, rows_ref, out_ref):
        rows = dot(place[512 * e : 512 * e + 512], rows_ref[...]).astype(BF16)
        out_ref[e] = rows.reshape(N_SX, CAP, 512)

    loads[6].wait()
    gather(0, cot_ref, csend)
    gather(1, cot_ref, csend)
    cots_out.start()
    for e in range(2):
        cotr[e, 0] = csend[e, me]

    lane = lax.shift_right_logical(lax.broadcasted_iota(jnp.int32, (256, 128), 1), 5)
    row = lax.shift_right_logical(
        jnp.bitwise_and(lax.broadcasted_iota(jnp.int32, (256, 128), 0), 127), 5
    )
    ones = jnp.where(lane == row, 1.0, 0.0).astype(BF16)

    for n in (0, 1, 7, 8):
        loads[n].wait()
    row_cut = jnp.where(sy == 0, 1, 0)
    for w in (1, 0):
        for piece in (1, 2) if w else (0, 4, 3):
            halo(piece, True).wait_recv()
        qkv[...] = dot(region[2 * w : 2 * w + 2].reshape(256, 512), wqkv[...])
        col_cut = jnp.where(me == 0, 1 - w, 0)

        def label(axis):
            b = lax.shift_right_logical(lax.broadcasted_iota(jnp.int32, (256, 256), axis), 6)
            return jnp.bitwise_and(b, 1) * (2 * row_cut) + lax.shift_right_logical(b, 1) * col_cut

        same = jnp.where(label(0) == label(1), 1.0, 0.0)

        def group(g, carry):
            attend_group(qkv, joined, g, scale_ref, ones, same)
            return carry

        lax.fori_loop(0, 4, group, 0)
        attended = dot(joined[...], wproj[...]).astype(BF16)
        attb[2 * w : 2 * w + 2] = attended.reshape(2, 2, 64, 512)
        for piece in (1, 2) if w else (0, 4, 3):
            halo(piece, False).start()
        for cg in (2, 3) if w else (1,):
            resid[tile_at(cg - 1, 0)] += attb[cg, 1].astype(F32).reshape(8, 8, 512)
    for piece in (1, 2, 0, 4, 3):
        cg, rh = places[piece]
        halo(piece, False).wait_recv()
        at = tile_at((cg + 3) % 4, 1 - rh)
        resid[at] += homeb[piece].astype(F32).reshape(8, 8, 512)
    for c in range(4):
        rows = layer_norm(resid[4 * c : 4 * c + 4].reshape(128, 512))
        normed2[128 * c : 128 * c + 128] = rows.astype(BF16)
    for e in range(2):
        gather(e, normed2, send)
        if e:
            rows_out[0].wait(send.at[0, others], xs.at[0])
        rows_out[e].start()
        recv[e, 0] = send[e, me]
    loads[2].wait()
    loads[3].wait()
    cots_out.wait(csend.at[:, others], cs.at[0])
    cots_out.wait(cotr.at[:, others], cr.at[0])

    def hidden_part(e):
        rows_out[e].wait(recv.at[e, others], xr.at[e])
        rows = recv[e].reshape(512, 512)
        logits = dot_nt(rows, router_ref[...])
        column = lax.broadcasted_iota(jnp.int32, logits.shape, 1) == 2 * me + e
        gate = jax.nn.sigmoid(jnp.sum(jnp.where(column, logits, 0.0), axis=1, keepdims=True))
        rgrad[e] = (gate * cotr[e].reshape(512, 512).astype(F32)).astype(BF16)
        rows_t[e] = rows.T

        def step(f, carry):
            part = pl.ds(pl.multiple_of(f * 256, 256), 256)
            act = dot(recv[e].reshape(512, 512), wup[e, :, part])
            hid, slope = gelu_parts(act)
            hidden[e, :, part] = hid.astype(BF16)
            through = dot_nt(rgrad[e], wdown[e, part, :])
            grad = (through * slope).astype(BF16)
            for n in range(2):
                col = (lax.rem(f, 2) * 2 + n) * 512 + (f // 2) * 128
                col = pl.multiple_of(col, 128)
                gact[e, :, pl.ds(col, 128)] = grad[:, 128 * n : 128 * n + 128]
            return carry

        lax.fori_loop(0, 8, step, 0)

    def return_part(e):
        out = dot(hidden[e], wdown[e]).astype(BF16)
        csend[e] = out.reshape(N_SX, CAP, 512)
        back[e, me] = csend[e, 0]

    def x_of(q):
        return (q % 2) * 2 + q // 2

    def halves_of(e):
        def fill_up(to, ix, rank_of):
            q = lax.rem(ix, 2) * 2 + ix // 2
            all_y = dot(rows_t[e], gact[e, :, pl.ds(pl.multiple_of(q * 512, 512), 512)])
            for iy in range(4):
                for h in range(2):
                    part = all_y[256 * h : 256 * h + 256, 128 * iy : 128 * iy + 128]
                    to[h, rank_of(iy)] = part.astype(BF16)

        def fill_down(to, iy, rank_of):
            hid = hidden[e, :, pl.ds(pl.multiple_of(iy * 512, 512), 512)]
            all_x = dot_tn(hid, rgrad[e])
            for q in range(4):
                for h in range(2):
                    part = all_x[128 * q : 128 * q + 128, 256 * h : 256 * h + 256]
                    to[h, rank_of(x_of(q))] = part.astype(BF16)

        up_refs = [ref.at[e] for ref in (us, u1, u2, uh) + sems[:4]]
        down_refs = [ref.at[e] for ref in (ds, d1, d2, dh) + sems[4:]]
        return (
            RingHalf(
                fill_up, x, y, to_x, to_y, up_refs, lambda h: oup_ref.at[e, pl.ds(256 * h, 256)]
            ),
            RingHalf(
                fill_down, y, x, to_y, to_x, down_refs,
                lambda h: odown_ref.at[e, :, pl.ds(256 * h, 256)],
            ),
        )

    first, second = halves_of(0), halves_of(1)

    def each(halves, method, *steps):
        for step in steps or ((),):
            for half in halves:
                getattr(half, method)(*step)

    hidden_part(0)
    each(first, "send_far")
    each(first, "send_raw")
    each(first, "pass_on", (0,), (1,))
    each(first, "keep_own")
    return_part(0)
    hidden_part(1)
    each(second, "send_far")
    each(second, "send_raw")
    each(first, "close1", (0,), (1,))
    return_part(1)
    home.start()
    each(second, "pass_on", (0,), (1,))
    each(first, "pass_on2")
    each(second, "keep_own")
    each(second, "close1", (0,), (1,))
    each(second, "pass_on2")
    logits = dot_nt(router_ref[...], normed2[...])
    gate = jax.nn.sigmoid(jnp.sum(jnp.where(named, logits, 0.0), axis=0, keepdims=True))
    same_token = lax.broadcasted_iota(jnp.int32, (512, 512), 0) == lax.broadcasted_iota(
        jnp.int32, (512, 512), 1
    )
    gate = jnp.sum(jnp.where(same_token, gate, 0.0), axis=1, keepdims=True)
    home.wait(back.at[:, others], br.at[0])
    moe = dot_tn(place[...], back[...].reshape(1024, 512))
    mixed_ref[...] = (resid[...].reshape(512, 512) + gate * moe).astype(BF16)
    for half in first + second:
        half.close2()
    for half in first + second:
        half.finish()
    rows_out[1].wait(send.at[1, others], xs.at[1])
    home.wait(csend.at[:, others], bs.at[0])
    for piece in range(5):
        halo(piece, True).wait_send()
        halo(piece, False).wait_send()


def on_device(tokens, cotangent, w_qkv, w_proj, logit_scale, w_router, w_up, w_down, expert_ids):
    dma = pltpu.SemaphoreType.DMA
    vmem = pl.BlockSpec(memory_space=pltpu.VMEM)
    hbm = pl.BlockSpec(memory_space=pltpu.HBM)
    ring = [dma((2,)), dma((2, 3, 2, 2)), dma((2,)), dma((2, 3, 2))]
    buffers = [
        ((16, 32, 512), BF16),
        ((512, 512), BF16),
        ((1, 512), jnp.int32),
        None,
        ((32, 512), BF16),
        ((512, 1536), BF16),
        ((512, 512), BF16),
        ((2, 512, 2048), BF16),
        ((2, 2048, 512), BF16),
        ((16, 32, 512), F32),
        ((5, 64, 512), BF16),
        ((4, 2, 64, 512), BF16),
        ((256, 1536), F32),
        ((256, 512), BF16),
        ((4, 2, 64, 512), BF16),
        ((5, 64, 512), BF16),
        ((1024, 512), BF16),
        ((512, 512), BF16),
        ((2, N_SX, CAP, 512), BF16),
        ((2, N_SX, CAP, 512), BF16),
        ((2, N_SX, CAP, 512), BF16),
        ((2, N_SX, CAP, 512), BF16),
        ((2, 512, 512), BF16),
        ((2, 512, 512), BF16),
        ((2, 512, 2048), BF16),
        ((2, 512, 2048), BF16),
        ((2, N_SX, CAP, 512), BF16),
        ((2, 4, 2, 4, 256, 128), BF16),
        ((2, 3, 2, 4, 256, 128), BF16),
        ((2, 3, 2, 256, 128), BF16),
        ((2, 3, 2, 256, 128), BF16),
        ((2, 4, 2, 4, 128, 256), BF16),
        ((2, 3, 2, 4, 128, 256), BF16),
        ((2, 3, 2, 128, 256), BF16),
        ((2, 3, 2, 128, 256), BF16),
    ]
    mixed, grad_up, grad_down = pl.pallas_call(
        block_kernel,
        out_shape=(
            jax.ShapeDtypeStruct((512, 512), BF16),
            jax.ShapeDtypeStruct((2, 512, 128), F32),
            jax.ShapeDtypeStruct((2, 128, 512), F32),
        ),
        in_specs=[hbm] * 9,
        out_specs=(vmem,) * 3,
        scratch_shapes=[pltpu.VMEM(*b) if b else pltpu.SMEM((16,), F32) for b in buffers]
        + [dma((9,))]
        + [dma((5,))] * 4
        + [dma((2,))] * 6
        + ring * 2,
        compiler_params=pltpu.CompilerParams(
            collective_id=0, has_side_effects=True, vmem_limit_bytes=VMEM_MIB * 1024 * 1024
        ),
        name="block",
    )(
        tokens[0],
        cotangent.reshape(512, 512),
        expert_ids.reshape(1, 512),
        logit_scale,
        w_router.T,
        w_qkv,
        w_proj,
        w_up,
        w_down,
    )
    return (mixed.reshape(1, 16, 32, 512), grad_up, grad_down)


def solution(mesh):
    return jax.shard_map(
        on_device,
        mesh=mesh,
        in_specs=(
            P("dp", "sy", "sx", None),
            P("dp", "sy", "sx", None),
            P(),
            P(),
            P(),
            P(),
            P("sx", None, None),
            P("sx", None, None),
            P("dp", "sy", "sx", None, None),
        ),
        out_specs=(
            P("dp", "sy", "sx", None),
            P("sx", None, ("sy", "dp")),
            P("sx", ("sy", "dp"), None),
        ),
        check_vma=False,
    )
```
